512 devices in a mesh: frame: 32 (over y, z_lo, core), tensor: 16 (over x, z_hi).
Axes of the slice: x: 4, y: 8, z: 8 (z_hi: 4, z_lo: 2; z = z_hi * 2 + z_lo), core: 2. Of those that a mesh axis runs over, the one named last changes fastest.
Arguments:
- frames_in: bfloat16 [32, 256, 2048], P('frame', None, 'tensor'), may hold values from -6 to 6
- spatial_gain: float32 [2048], replicated, may hold values from 0.25 to 1.75
- spatial_qkv: bfloat16 [2048, 3, 2048], P('frame', None, 'tensor'), may hold values from -0.125 to 0.125
- spatial_out: bfloat16 [2048, 2048], P('frame', 'tensor'), may hold values from -0.125 to 0.125
- spatial_up: bfloat16 [2048, 4096], P('frame', 'tensor'), may hold values from -0.125 to 0.125
- spatial_down: bfloat16 [2048, 4096], P('frame', 'tensor'), may hold values from -0.09375 to 0.09375
- temporal_gain: float32 [2048], replicated, may hold values from 0.25 to 1.75
- temporal_qkv: bfloat16 [2048, 3, 2048], P('frame', None, 'tensor'), may hold values from -0.125 to 0.125
- temporal_out: bfloat16 [2048, 2048], P('frame', 'tensor'), may hold values from -0.125 to 0.125
- temporal_up: bfloat16 [2048, 4096], P('frame', 'tensor'), may hold values from -0.125 to 0.125
- temporal_down: bfloat16 [2048, 4096], P('frame', 'tensor'), may hold values from -0.09375 to 0.09375
Outputs:
- encoded: bfloat16 [32, 256, 2048], P(None, 'frame', 'tensor')
The draws below stay inside these ranges and needn't reach their ends.
All inputs are finite; a program needn't handle non-finite values.
Results may differ from the reference program's by a relative error of at most 0.022.
Values may be sent and summed in bfloat16 or wider, within the bound.
A program may use at most 64 MiB of HBM per device.

```python
import jax
import jax.numpy as jnp
from jax import lax

D = 2048
HEADS = 16
HEAD_DIM = 128
FF = 4096
PATCHES = 256
FRAMES = 32
N_TENSOR = 16


def steps_of(rng, extent, split, least, top_value):
    factor_of, own = 1.0, jax.random.fold_in(rng, 6)
    for axis_at, shards_of in split:
        steps = jnp.exp(jax.random.uniform(jax.random.fold_in(own, axis_at), (shards_of,), jnp.float32, least / len(split), top_value / len(split)))
        factor_of = factor_of * jnp.repeat(steps, extent[axis_at] // shards_of).reshape([-1 if axis == axis_at else 1 for axis in range(len(extent))])
    return factor_of


def noise(stream_key, shape, scale, bound, pieces=(), dtype=jnp.bfloat16):
    drawn = jax.random.normal(stream_key, shape, jnp.float32) * scale
    if len(pieces) > 0:
        drawn = steps_of(stream_key, shape, pieces, -0.22, 0.18) * drawn
    return jnp.clip(drawn, min=-bound, max=bound).astype(dtype)


def setup_inputs(seed: int = 0) -> dict:
    key_of = jax.random.split(jax.random.key(seed), 12)
    return {
        "frames_in": noise(key_of[0], (FRAMES, PATCHES, D), 1.0, 6.0, ((0, 32), (2, 16))),
        "spatial_gain": jnp.clip(1.0 + 0.15 * jax.random.normal(key_of[1], (D,), jnp.float32), 0.25, 1.75),
        "spatial_qkv": noise(key_of[2], (D, 3, D), D ** -0.5, 0.125, ((0, 32), (2, 16))),
        "spatial_out": noise(key_of[3], (D, D), D ** -0.5, 0.125, ((0, 32), (1, 16))),
        "spatial_up": noise(key_of[4], (D, FF), D ** -0.5, 0.125, ((0, 32), (1, 16))),
        "spatial_down": noise(key_of[5], (D, FF), FF ** -0.5, 0.09375, ((0, 32), (1, 16))),
        "temporal_gain": jnp.clip(1.0 + 0.15 * jax.random.normal(key_of[6], (D,), jnp.float32), 0.25, 1.75),
        "temporal_qkv": noise(key_of[7], (D, 3, D), D ** -0.5, 0.125, ((0, 32), (2, 16))),
        "temporal_out": noise(key_of[8], (D, D), D ** -0.5, 0.125, ((0, 32), (1, 16))),
        "temporal_up": noise(key_of[9], (D, FF), D ** -0.5, 0.125, ((0, 32), (1, 16))),
        "temporal_down": noise(key_of[10], (D, FF), FF ** -0.5, 0.09375, ((0, 32), (1, 16))),
    }


EPS = 1e-06

def norm_rows(values, gain):
    centered = values - lax.optimization_barrier(jnp.mean(values, axis=-1, keepdims=True))
    spread = lax.optimization_barrier(jnp.mean(centered * centered, axis=-1, keepdims=True))
    return centered * lax.rsqrt(spread + EPS) * gain

def attend(qkv, time_major):
    query = norm_rows(qkv[:, :, 0], 1.0).astype(jnp.bfloat16).astype(jnp.float32)
    keys = norm_rows(qkv[:, :, 1], 1.0).astype(jnp.bfloat16).astype(jnp.float32)
    values = qkv[:, :, 2].astype(jnp.bfloat16).astype(jnp.float32)
    if time_major:
        first, second = ('qbhd,kbhd->bhqk', 'bhqk,kbhd->qbhd')
    else:
        first, second = ('bqhd,bkhd->bhqk', 'bhqk,bkhd->bqhd')
    scores = jnp.einsum(first, query, keys) * qkv.shape[-1] ** (-0.5)
    expo = jnp.exp(scores)
    weights = (expo / lax.optimization_barrier(jnp.sum(expo, axis=-1, keepdims=True))).astype(jnp.bfloat16)
    return jnp.einsum(second, weights.astype(jnp.float32), values).astype(jnp.bfloat16)

def block(inputs, gain, qkv_weight, out_weight, up_weight, down_weight, time_major):
    first, second, width = inputs.shape
    normed = norm_rows(inputs.astype(jnp.float32), gain.astype(jnp.float32)).astype(jnp.bfloat16)
    flat = normed.reshape(-1, width)
    qkv = jnp.dot(flat, qkv_weight.reshape(width, -1), preferred_element_type=jnp.float32)
    qkv = qkv.reshape(first, second, 3, HEADS, HEAD_DIM)
    mixed = attend(qkv, time_major).reshape(-1, width)
    hidden = jax.nn.gelu(jnp.dot(flat, up_weight, preferred_element_type=jnp.float32), approximate=True).astype(jnp.bfloat16)
    head_cols = width // N_TENSOR
    unit_cols = FF // N_TENSOR
    contract = (((1,), (1,)), ((), ()))
    total = jnp.zeros((flat.shape[0], width), jnp.float32)
    for group in range(N_TENSOR):
        hs = slice(group * head_cols, (group + 1) * head_cols)
        us = slice(group * unit_cols, (group + 1) * unit_cols)
        term = lax.dot_general(mixed[:, hs], out_weight[:, hs], contract, preferred_element_type=jnp.float32)
        term = term + lax.dot_general(hidden[:, us], down_weight[:, us], contract, preferred_element_type=jnp.float32)
        term = lax.optimization_barrier(term.astype(jnp.bfloat16)).astype(jnp.float32)
        total = total + term
    return (inputs.astype(jnp.float32) + total.reshape(first, second, width)).astype(jnp.bfloat16)

def reference(frames_in, spatial_gain, spatial_qkv, spatial_out, spatial_up, spatial_down, temporal_gain, temporal_qkv, temporal_out, temporal_up, temporal_down):
    middle = block(frames_in, spatial_gain, spatial_qkv, spatial_out, spatial_up, spatial_down, False)
    return block(middle, temporal_gain, temporal_qkv, temporal_out, temporal_up, temporal_down, True)
```

```python
import jax
import jax.numpy as jnp
from jax import lax
from jax.experimental import pallas as pl
from jax.experimental.pallas import tpu as pltpu
from jax.sharding import PartitionSpec as P

MESH = pl.DeviceIdType.MESH
EPS = 1e-06
BF = jnp.bfloat16
F32 = jnp.float32
NT = (((1,), (1,)), ((), ()))


def norm_rows(values):
    centered = values - jnp.mean(values, axis=-1, keepdims=True)
    spread = jnp.mean(centered * centered, axis=-1, keepdims=True)
    return centered * lax.rsqrt(spread + EPS)


def kernel(
    x_in, gain1, gain2, qkv1, out1, up1, down1, qkv2, out2, up2, down2,
    y_out,
    w, xs, h, terms, from_x, to_z, from_z, mid, turned,
    local_sem, w_send, w_recv, ag_send, ag_recv, rx_send, rx_recv, rz_send, rz_recv, turn_send, turn_recv,
):
    f, t = lax.axis_index("frame"), lax.axis_index("tensor")
    xi, zh = t // 4, t % 4
    f_z = (f // 4) * 4 + (f + 2) % 4
    f_core = f + 1 - 2 * (f % 2)
    f_up, f_down = (f + 4) % 32, (f + 28) % 32

    def tensor_at(dx, dz):
        return ((xi + dx) % 4) * 4 + (zh + dz) % 4

    pending = []

    def send(src, dst, send_sem, recv_sem, device):
        copy = pltpu.make_async_remote_copy(src, dst, send_sem, recv_sem, device_id=device, device_id_type=MESH)
        copy.start()
        pending.append(copy)

    def arrived(dst, recv_sem):
        pltpu.make_async_remote_copy(dst, dst, recv_sem, recv_sem, device_id=(f_core, t), device_id_type=MESH).wait_recv()

    local = [pltpu.make_async_copy(x_in, xs.at[0, t], local_sem.at[12])]
    for b, (qkv, up, out, down) in enumerate(((qkv1, up1, out1, down1), (qkv2, up2, out2, down2))):
        parts = [(qkv.at[j], 128 * j, 128) for j in range(3)] + [(up, 384, 256), (out, 640, 128), (down, 768, 256)]
        for i, (ref, at, width) in enumerate(parts):
            local.append(pltpu.make_async_copy(ref, w.at[b, f, :, pl.ds(at, width)], local_sem.at[6 * b + i]))
    for copy in local:
        copy.start()

    barrier = pltpu.get_barrier_semaphore()
    peers = [(f_z, t), (f_core, t), (f_up, t), (f_down, t)]
    peers += [(f, tensor_at(dx, 0)) for dx in (1, 2, 3)] + [(f, tensor_at(0, dz)) for dz in (1, 2, 3)]
    for peer in peers:
        pl.semaphore_signal(barrier, inc=1, device_id=peer, device_id_type=MESH)
    for copy in local:
        copy.wait()
    pl.semaphore_wait(barrier, len(peers))

    used = [0, 0]

    def w_push(b, slot, target):
        send(w.at[b, slot], w.at[b, slot], w_send.at[b, used[b]], w_recv.at[b, slot], (target, t))
        used[b] += 1

    def w_wait(b, slot):
        arrived(w.at[b, slot], w_recv.at[b, slot])

    def w_own(b):
        w_push(b, f, f_z)
        w_push(b, f, f_up)
        w_push(b, f, f_down)
        w_push(b, f, f_core)

    def w_pair(b):
        w_wait(b, f_z)
        w_push(b, f_z, f_up)
        w_push(b, f_z, f_down)
        w_push(b, f_z, f_core)

    def w_hop(b, hop):
        below = [(f + 32 - 4 * hop) % 32, (f_z + 32 - 4 * hop) % 32]
        above = [(f + 4 * hop) % 32, (f_z + 4 * hop) % 32]
        for i in range(2):
            w_wait(b, below[i])
            if hop < 3 or i == 0:
                w_push(b, below[i], f_up)
            w_push(b, below[i], f_core)
            w_wait(b, above[i])
            if hop < 3 or i == 1:
                w_push(b, above[i], f_down)
            w_push(b, above[i], f_core)

    def w_last(b):
        for slot in ((f + 16) % 32, (f_z + 16) % 32):
            w_wait(b, slot)
            w_push(b, slot, f_core)

    def w_core(b):
        for k in range(8):
            w_wait(b, (f_core + 4 * k) % 32)
            w_wait(b, (f_core // 4 * 4 + (f_core + 2) % 4 + 4 * k) % 32)

    def gather_push(b, dx, dz, to_dx, to_dz):
        slot = tensor_at(4 - dx, 4 - dz)
        rel = (dx + to_dx) * 4 + dz + to_dz
        send(xs.at[b, slot], xs.at[b, slot], ag_send.at[b, rel], ag_recv.at[b, rel], (f, tensor_at(to_dx, to_dz)))

    def gather_wait(b, dx, dz):
        arrived(xs.at[b, tensor_at(4 - dx, 4 - dz)], ag_recv.at[b, dx * 4 + dz])

    def gather_own(b):
        for dz in (2, 1, 3):
            gather_push(b, 0, 0, 0, dz)
        for dx in (2, 1, 3):
            gather_push(b, 0, 0, dx, 0)

    def gather_forward(b, dz):
        gather_wait(b, 0, dz)
        for dx in (2, 1, 3):
            gather_push(b, 0, dz, dx, 0)

    def gather_rest(b):
        for dz in (0, 1, 3, 2):
            for dx in (1, 2, 3):
                gather_wait(b, dx, dz)

    def normalize(b):
        total = xs[b, 0].astype(F32)
        for i in range(1, 16):
            total += xs[b, i].astype(F32)
        mean = jnp.sum(total, axis=-1, keepdims=True) * (1.0 / 2048)
        square = jnp.zeros((256, 128), F32)
        for i in range(16):
            centered = xs[b, i].astype(F32) - mean
            square += centered * centered
        scale = lax.rsqrt(jnp.sum(square, axis=-1, keepdims=True) * (1.0 / 2048) + EPS)
        for i in range(16):
            centered = xs[b, i].astype(F32) - mean
            h[:, 128 * i : 128 * (i + 1)] = (centered * scale * (gain1, gain2)[b][i]).astype(BF)

    def inner(b):
        mixed = jnp.dot(h[...], w[b, :, :, 0:640].reshape(2048, 640), preferred_element_type=F32)
        query = norm_rows(mixed[:, 0:128]).astype(BF)
        keys = norm_rows(mixed[:, 128:256]).astype(BF)
        scores = lax.dot_general(query, keys, NT, preferred_element_type=F32) * 128**-0.5
        expo = jnp.exp(scores)
        if b == 1:
            row = lax.broadcasted_iota(jnp.int32, (256, 256), 0)
            col = lax.broadcasted_iota(jnp.int32, (256, 256), 1)
            expo = jnp.where(row % 8 == col % 8, expo, 0.0)
        weights = (expo * (1.0 / jnp.sum(expo, axis=-1, keepdims=True))).astype(BF)
        attended = jnp.dot(weights, mixed[:, 256:384].astype(BF), preferred_element_type=F32).astype(BF)
        hidden = jax.nn.gelu(mixed[:, 384:640], approximate=True).astype(BF)
        return jnp.concatenate([attended, hidden], axis=1)

    order = (2, 1, 3, 0)

    def project(b, both):
        for dz in order:
            for dx in (2, 1, 3, 0):
                slot = 2 * tensor_at(dx, dz)
                piece = w[b, pl.ds(slot, 2), :, 640:1024].reshape(128, 384)
                terms[b, dx, dz] = lax.dot_general(both, piece, NT, preferred_element_type=F32).astype(BF)
                if dx:
                    send(
                        terms.at[b, dx, dz], from_x.at[b, dx - 1, dz], rx_send.at[b, dx - 1, dz],
                        rx_recv.at[b, dx - 1, dz], (f, tensor_at(dx, 0)),
                    )

    def reduce(b):
        total = None
        for dz in order:
            total = terms[b, 0, dz].astype(F32)
            for i in range(3):
                arrived(from_x.at[b, i, dz], rx_recv.at[b, i, dz])
                total += from_x[b, i, dz].astype(F32)
            if dz:
                to_z[b, dz - 1] = total.astype(BF)
                send(
                    to_z.at[b, dz - 1], from_z.at[b, dz - 1], rz_send.at[b, dz - 1], rz_recv.at[b, dz - 1],
                    (f, tensor_at(0, dz)),
                )
        for i in (0, 2, 1):
            arrived(from_z.at[b, i], rz_recv.at[b, i])
            total += from_z[b, i].astype(F32)
        return total

    def turn(middle):
        mid[...] = middle.reshape(32, 8, 128)
        for i in range(1, 32):
            to = (f + i) % 32
            send(mid.at[to], turned.at[f], turn_send.at[i - 1], turn_recv.at[i - 1], (to, t))
        turned[f] = mid[f]
        for i in range(1, 32):
            arrived(turned.at[(f + 32 - i) % 32], turn_recv.at[i - 1])

    gather_own(0)
    w_own(0)
    w_pair(0)
    for dz in (1, 3, 2):
        gather_forward(0, dz)
    w_hop(0, 1)
    w_hop(0, 2)
    w_hop(0, 3)
    w_own(1)
    gather_rest(0)
    normalize(0)
    w_last(0)
    w_pair(1)
    w_core(0)
    both = inner(0)
    project(0, both)
    w_hop(1, 1)
    share = reduce(0)
    middle = (xs[0, t].astype(F32) + share).astype(BF).astype(F32)
    turn(middle)
    xs[1, t] = turned[...].reshape(256, 128).astype(BF)
    gather_own(1)
    w_hop(1, 2)
    for dz in (1, 3, 2):
        gather_forward(1, dz)
    w_hop(1, 3)
    w_last(1)
    gather_rest(1)
    normalize(1)
    w_core(1)
    both = inner(1)
    project(1, both)
    share = reduce(1)
    y_out[...] = (turned[...].reshape(256, 128) + share).astype(BF)
    for copy in pending:
        copy.wait_send()


def body(
    frames_in,
    spatial_gain,
    spatial_qkv,
    spatial_out,
    spatial_up,
    spatial_down,
    temporal_gain,
    temporal_qkv,
    temporal_out,
    temporal_up,
    temporal_down,
):
    dma = pltpu.SemaphoreType.DMA
    result = pl.pallas_call(
        kernel,
        out_shape=jax.ShapeDtypeStruct((256, 128), BF),
        in_specs=[pl.BlockSpec(memory_space=pl.ANY), pl.BlockSpec(memory_space=pltpu.VMEM), pl.BlockSpec(memory_space=pltpu.VMEM)]
        + [pl.BlockSpec(memory_space=pl.ANY)] * 8,
        out_specs=pl.BlockSpec(memory_space=pltpu.VMEM),
        scratch_shapes=[
            pltpu.VMEM((2, 32, 64, 1024), BF),
            pltpu.VMEM((2, 16, 256, 128), BF),
            pltpu.VMEM((256, 2048), BF),
            pltpu.VMEM((2, 4, 4, 256, 128), BF),
            pltpu.VMEM((2, 3, 4, 256, 128), BF),
            pltpu.VMEM((2, 3, 256, 128), BF),
            pltpu.VMEM((2, 3, 256, 128), BF),
            pltpu.VMEM((32, 8, 128), F32),
            pltpu.VMEM((32, 8, 128), F32),
            dma((13,)),
            dma((2, 31)),
            dma((2, 32)),
            dma((2, 16)),
            dma((2, 16)),
            dma((2, 3, 4)),
            dma((2, 3, 4)),
            dma((2, 3)),
            dma((2, 3)),
            dma((31,)),
            dma((31,)),
        ],
        compiler_params=pltpu.CompilerParams(collective_id=0, has_side_effects=True, vmem_limit_bytes=63 << 20),
    )(
        frames_in.reshape(256, 128),
        spatial_gain.reshape(16, 1, 128),
        temporal_gain.reshape(16, 1, 128),
        jnp.transpose(spatial_qkv, (1, 0, 2)),
        spatial_out,
        spatial_up,
        spatial_down,
        jnp.transpose(temporal_qkv, (1, 0, 2)),
        temporal_out,
        temporal_up,
        temporal_down,
    )
    return result.reshape(32, 8, 128)


def solution(mesh):
    in_specs = (
        P("frame", None, "tensor"),
        P(),
        P("frame", None, "tensor"),
        P("frame", "tensor"),
        P("frame", "tensor"),
        P("frame", "tensor"),
        P(),
        P("frame", None, "tensor"),
        P("frame", "tensor"),
        P("frame", "tensor"),
        P("frame", "tensor"),
    )
    out_specs = P(None, "frame", "tensor")
    return jax.shard_map(body, mesh=mesh, in_specs=in_specs, out_specs=out_specs, check_vma=False)
```

```python
import jax
import jax.numpy as jnp
from jax import lax
from jax.experimental import pallas as pl
from jax.experimental.pallas import tpu as pltpu
from jax.sharding import PartitionSpec as P

MESH = pl.DeviceIdType.MESH
EPS = 1e-06
BF = jnp.bfloat16
F32 = jnp.float32
NT = (((1,), (1,)), ((), ()))
PARTS = 2
EACH = 8 // PARTS
ROWS = 32 * EACH
EACH_BITS, ROWS_BITS = EACH.bit_length() - 1, ROWS.bit_length() - 1
PIECES = (4, 2)


def norm_rows(values):
    centered = values - jnp.mean(values, axis=-1, keepdims=True)
    spread = jnp.mean(centered * centered, axis=-1, keepdims=True)
    return centered * lax.rsqrt(spread + EPS)


def kernel(
    x_in, gain1_in, gain2_in, qkv1, out1, up1, down1, qkv2, out2, up2, down2,
    y_out,
    w, gain1, gain2, x_own, xs, xt, h, terms, from_x, to_z, from_z, mid, turned, ready,
    local_sem, w_send, w_early, w_late, w_last, ag_send, ag_recv, rx_send, rx_recv, rz_send, rz_recv, turn_send, turn_recv,
):
    f, t = lax.axis_index("frame"), lax.axis_index("tensor")
    xi, zh = t // 4, t % 4
    odd, lo = f % 2, (f // 2) % 2
    f_z = (f // 4) * 4 + (f + 2) % 4
    f_core = f + 1 - 2 * odd

    def at_y(base, r):
        return (base + 4 * (r % 8)) % 32

    def tensor_at(dx, dz):
        return ((xi + dx) % 4) * 4 + (zh + dz) % 4

    def send(src, dst, send_sem, recv_sem, device):
        pltpu.make_async_remote_copy(src, dst, send_sem, recv_sem, device_id=device, device_id_type=MESH).start()

    def arrived(ref, sem):
        pltpu.make_async_remote_copy(ref, ref, sem, sem, device_id=(f_core, t), device_id_type=MESH).wait_recv()

    def left(ref, sem):
        pltpu.make_async_remote_copy(ref, ref, sem, sem, device_id=(f_core, t), device_id_type=MESH).wait_send()

    def part_order(axis):
        shapes = [(256, 1), (1, 256)]
        part = lax.broadcasted_iota(jnp.int32, shapes[axis], axis)
        own = lax.broadcasted_iota(jnp.int32, shapes[1 - axis], 1 - axis)
        natural = ((part & (ROWS - 1)) >> EACH_BITS << 3) + (part >> ROWS_BITS << EACH_BITS) + (part & (EACH - 1))
        return jnp.where(natural == own, 1.0, 0.0).astype(BF)

    pltpu.make_async_copy(x_in, x_own, local_sem.at[0]).start()
    pltpu.make_async_copy(gain1_in, gain1, local_sem.at[1]).start()
    pltpu.make_async_copy(gain2_in, gain2, local_sem.at[2]).start()
    for b, (qkv, up, out, down) in enumerate(((qkv1, up1, out1, down1), (qkv2, up2, out2, down2))):
        for ref, at, width in [(qkv.at[j], 128 * j, 128) for j in range(3)] + [(up, 384, 256), (out, 640, 128), (down, 768, 256)]:
            pltpu.make_async_copy(ref, w.at[b, f, :, pl.ds(at, width)], local_sem.at[3 + b]).start()

    def placed(ref, k):
        pltpu.make_async_copy(ref, ref, local_sem.at[k]).wait()

    barrier = pltpu.get_barrier_semaphore()
    peers = [(f_z, t), (f_core, t), (at_y(f, 1), t), (at_y(f, -1), t)]
    peers += [(f, tensor_at(dx, 0)) for dx in (1, 2, 3)] + [(f, tensor_at(0, dz)) for dz in (1, 2, 3)]
    for peer in peers:
        pl.semaphore_signal(barrier, inc=1, device_id=peer, device_id_type=MESH)
    placed(x_own, 0)
    placed(w.at[0, f], 3)
    xs[t] = jnp.dot(part_order(0), x_own[...], preferred_element_type=F32).astype(BF)
    pl.semaphore_wait(barrier, len(peers))

    used = [0, 0]

    def piece(b, i, slot):
        rows = 64 // PIECES[b]
        return w.at[b, slot, pl.ds(i * rows, rows), :]

    def w_sem(b, i, kind):
        return w_late.at[i, kind] if b else w_early.at[i, kind]

    def w_push(b, i, slot, target, kind=None):
        used[b] += 1
        send(piece(b, i, slot), piece(b, i, slot), w_send.at[b], w_last.at[b] if kind is None else w_sem(b, i, kind), (target, t))

    def w_first(b, i):
        w_push(b, i, f, f_z, 4)
        w_push(b, i, f, at_y(f, 1), 0)
        w_push(b, i, f, at_y(f, -1), 0)
        w_push(b, i, f, f_core)

    def w_rank(b, i, own, k):
        base = f if own else f_z
        early = i < PIECES[b] // 2
        kind = k - 1 if own else 4 + k
        rows = 64 // PIECES[b]
        both = k in (1, 2, 3)
        arrived(w.at[b, pl.ds(0, 2), pl.ds(0, rows), :] if both else piece(b, i, at_y(base, k)), w_sem(b, i, kind))
        for r in (-k, k) if both else (k,):
            slot = at_y(base, r)
            if own or early:
                if r in (-2, -1, 0):
                    w_push(b, i, slot, at_y(f, 1), kind + 1)
                if r in (0, 1, 2):
                    w_push(b, i, slot, at_y(f, -1), kind + 1)
                if early and r == (-3 if own else 3):
                    w_push(b, i, slot, at_y(f, 1 if own else -1), kind + 1)
            if own and not early:
                if r == 3:
                    w_push(b, i, at_y(f, -3 + 6 * odd), at_y(f, 1 - 2 * odd), kind + 1)
                w_push(b, i, slot, f_z, 4 + k)
            w_push(b, i, slot, f_core)

    def w_core(b):
        arrived(w.at[b, pl.ds(0, 16)], w_last.at[b])

    def gather_push(view, k, dx, dz, to_dx, to_dz):
        slot = view.at[tensor_at(4 - dx, 4 - dz)]
        send(slot, slot, ag_send.at[k], ag_recv.at[k, to_dz], (f, tensor_at(to_dx, to_dz)))

    def gather_own(view, k):
        for dz in (2, 1, 3):
            gather_push(view, k, 0, 0, 0, dz)
        for dx in (2, 1, 3):
            gather_push(view, k, 0, 0, dx, 0)

    def gather_forward(view, k, dz):
        arrived(view.at[tensor_at(0, 4 - dz)], ag_recv.at[k, dz])
        for dx in (2, 1, 3):
            gather_push(view, k, 0, dz, dx, 0)

    def gather_rest(view, k):
        arrived(view.at[pl.ds(0, 12)], ag_recv.at[k, 0])

    def normalize(view, rows, gain):
        total = view[0].astype(F32)
        for i in range(1, 16):
            total += view[i].astype(F32)
        mean = jnp.sum(total, axis=-1, keepdims=True) * (1.0 / 2048)
        square = jnp.zeros((rows, 128), F32)
        for i in range(16):
            centered = view[i].astype(F32) - mean
            square += centered * centered
        scale = lax.rsqrt(jnp.sum(square, axis=-1, keepdims=True) * (1.0 / 2048) + EPS)
        for i in range(16):
            centered = view[i].astype(F32) - mean
            h[0:rows, 128 * i : 128 * (i + 1)] = (centered * scale * gain[i]).astype(BF)

    def inner(b, rows):
        mixed = jnp.dot(h[0:rows, :], w[b, :, :, 0:640].reshape(2048, 640), preferred_element_type=F32)
        query = norm_rows(mixed[:, 0:128]).astype(BF)
        keys = norm_rows(mixed[:, 128:256]).astype(BF)
        scores = lax.dot_general(query, keys, NT, preferred_element_type=F32) * 128**-0.5
        expo = jnp.exp(scores)
        if b == 1:
            row = lax.broadcasted_iota(jnp.int32, (rows, 1), 0)
            col = lax.broadcasted_iota(jnp.int32, (1, rows), 1)
            expo = jnp.where((row & (EACH - 1)) == (col & (EACH - 1)), expo, 0.0)
        weights = (expo * (1.0 / jnp.sum(expo, axis=-1, keepdims=True))).astype(BF)
        attended = jnp.dot(weights, mixed[:, 256:384].astype(BF), preferred_element_type=F32).astype(BF)
        hidden = jax.nn.gelu(mixed[:, 384:640], approximate=True).astype(BF)
        return jnp.concatenate([attended, hidden], axis=1)

    order = (2, 1, 3, 0)

    groups = []

    def project(b, k, dz, both):
        n = len(groups)
        if n >= 2:
            left(from_x.at[0, 0, 0], rx_send.at[n % 2])
        for dx in (2, 1, 3, 0):
            slot = 2 * tensor_at(dx, dz)
            weight = w[b, pl.ds(slot, 2), :, 640:1024].reshape(128, 384)
            terms[b, k, dx, dz] = lax.dot_general(both, weight, NT, preferred_element_type=F32).astype(BF)
            if dx:
                send(terms.at[b, k, dx, dz], from_x.at[b, k, dz, dx - 1], rx_send.at[n % 2], rx_recv.at[b, k, dz], (f, tensor_at(dx, 0)))
        groups.append(n)

    def sum_x(b, k, dz):
        arrived(from_x.at[b, k, dz], rx_recv.at[b, k, dz])
        total = terms[b, k, 0, dz].astype(F32)
        for i in range(3):
            total += from_x[b, k, dz, i].astype(F32)
        if dz:
            to_z[b, k, dz - 1] = total.astype(BF)
            send(to_z.at[b, k, dz - 1], from_z.at[b, k, dz - 1], rz_send.at[0], rz_recv.at[b, k], (f, tensor_at(0, dz)))
        else:
            ready[b, k] = total

    def sum_z(b, k):
        arrived(from_z.at[b, k], rz_recv.at[b, k])
        total = ready[b, k]
        for i in range(3):
            total += from_z[b, k, i].astype(F32)
        return total

    distances = sorted(range(1, 32), key=lambda i: -min(i // 4, 8 - i // 4))

    def turn(k):
        middle = (xs[t, k * ROWS : (k + 1) * ROWS, :].astype(F32) + sum_z(0, k)).astype(BF).astype(F32)
        mid[k] = middle.reshape(32, EACH, 128)
        for i in distances:
            to = (f + i) % 32
            send(mid.at[k, to], turned.at[k, f], turn_send.at[k], turn_recv.at[k], (to, t))
        turned[k, f] = mid[k, f]

    def turn_done(k):
        arrived(turned.at[k, pl.ds(0, 31)], turn_recv.at[k])
        xt[k, t] = turned[k].reshape(ROWS, 128).astype(BF)

    quarters = range(PIECES[0])
    for i in quarters[:1]:
        w_first(0, i)
    gather_own(xs, 0)
    for i in quarters[1:]:
        w_first(0, i)
    for i in quarters:
        w_rank(0, i, True, 1)
    for i in quarters:
        w_rank(0, i, False, 0)
    for i in (0, 1):
        w_rank(0, i, True, 2)
    gather_forward(xs, 0, 3 - 2 * lo)
    for i in (2, 3):
        w_rank(0, i, True, 2)
    for i in quarters:
        w_rank(0, i, False, 1)
    for i in (0, 1):
        w_rank(0, i, True, 3)
    gather_forward(xs, 0, 1 + 2 * lo)
    w_rank(0, 2, True, 3)
    gather_forward(xs, 0, 2)
    w_rank(0, 2, False, 2)
    w_rank(0, 3, True, 3)
    w_rank(0, 3, False, 2)
    for i in (0, 1):
        w_rank(0, i, False, 2)
    for i in quarters:
        w_rank(0, i, True, 4)
    for i in (2, 3, 0, 1):
        w_rank(0, i, False, 3)
    w_rank(0, 2, False, 4)
    gather_rest(xs, 0)
    placed(gain1, 1)
    normalize(xs, 256, gain1)
    for i in (3, 0, 1):
        w_rank(0, i, False, 4)

    def second(k):
        for i in range(PIECES[1]):
            if 0 < k < 5:
                w_rank(1, i, True, k)
            if k > 0:
                w_rank(1, i, False, k - 1)
            else:
                w_first(1, i)

    blocks = [(k, dz) for k in range(PARTS) for dz in order]

    def branch(b, rows_of, after_sum):
        issued = 0
        for i, (k, dz) in enumerate(blocks):
            for ahead in blocks[issued : i + 4]:
                project(b, *ahead, rows_of(*ahead))
                issued += 1
            sum_x(b, k, dz)
            after_sum(k, dz)

    w_core(0)
    both = inner(0, 256)
    placed(w.at[1, f], 4)
    placed(gain2, 2)
    second(0)

    def turn_last(k, dz):
        if k and dz == order[1]:
            turn(k - 1)

    branch(0, lambda k, dz: both[k * ROWS : (k + 1) * ROWS], turn_last)
    second(1)
    turn(PARTS - 1)
    for k in range(PARTS):
        turn_done(k)
        gather_own(xt.at[k], k + 1)
        if k == 0:
            second(2)
    for k in range(PARTS):
        for dz in (1, 3, 2):
            gather_forward(xt.at[k], k + 1, dz)
        if k == 0:
            second(3)
            second(4)

    rows2 = {}

    def enter(k, dz):
        if k not in rows2:
            gather_rest(xt.at[k], k + 1)
            normalize(xt.at[k], ROWS, gain2)
            if k == 0:
                second(5)
                w_core(1)
            rows2[k] = inner(1, ROWS)
        return rows2[k]

    branch(1, enter, lambda k, dz: None)
    total = jnp.concatenate([sum_z(1, k) for k in range(PARTS)], axis=0)
    kept = jnp.concatenate([turned[k].reshape(ROWS, 128) for k in range(PARTS)], axis=0)
    y_out[...] = jnp.dot(part_order(1), (kept + total).astype(BF), preferred_element_type=F32).astype(BF)
    for b in range(2):
        left(w.at[b, pl.ds(0, used[b] // PIECES[b])], w_send.at[b])
        left(from_x.at[0, 0, 0], rx_send.at[b])
    left(xs.at[pl.ds(0, 15)], ag_send.at[0])
    for k in range(PARTS):
        left(xt.at[k, pl.ds(0, 15)], ag_send.at[k + 1])
        left(mid.at[k, pl.ds(0, 31)], turn_send.at[k])
    left(to_z, rz_send.at[0])


def body(
    frames_in,
    spatial_gain,
    spatial_qkv,
    spatial_out,
    spatial_up,
    spatial_down,
    temporal_gain,
    temporal_qkv,
    temporal_out,
    temporal_up,
    temporal_down,
):
    dma = pltpu.SemaphoreType.DMA
    result = pl.pallas_call(
        kernel,
        out_shape=jax.ShapeDtypeStruct((256, 128), BF),
        in_specs=[pl.BlockSpec(memory_space=pl.ANY)] * 11,
        out_specs=pl.BlockSpec(memory_space=pltpu.VMEM),
        scratch_shapes=[
            pltpu.VMEM((2, 32, 64, 1024), BF),
            pltpu.VMEM((16, 1, 128), F32),
            pltpu.VMEM((16, 1, 128), F32),
            pltpu.VMEM((256, 128), BF),
            pltpu.VMEM((16, 256, 128), BF),
            pltpu.VMEM((PARTS, 16, ROWS, 128), BF),
            pltpu.VMEM((256, 2048), BF),
            pltpu.VMEM((2, PARTS, 4, 4, ROWS, 128), BF),
            pltpu.VMEM((2, PARTS, 4, 3, ROWS, 128), BF),
            pltpu.VMEM((2, PARTS, 3, ROWS, 128), BF),
            pltpu.VMEM((2, PARTS, 3, ROWS, 128), BF),
            pltpu.VMEM((PARTS, 32, EACH, 128), F32),
            pltpu.VMEM((PARTS, 32, EACH, 128), F32),
            pltpu.VMEM((2, PARTS, ROWS, 128), F32),
            dma((5,)),
            dma((2,)),
            dma((PIECES[0], 9)),
            dma((PIECES[1], 9)),
            dma((2,)),
            dma((1 + PARTS,)),
            dma((1 + PARTS, 4)),
            dma((2,)),
            dma((2, PARTS, 4)),
            dma((1,)),
            dma((2, PARTS)),
            dma((PARTS,)),
            dma((PARTS,)),
        ],
        compiler_params=pltpu.CompilerParams(collective_id=0, has_side_effects=True, vmem_limit_bytes=63 << 20),
    )(
        frames_in.reshape(256, 128),
        spatial_gain.reshape(16, 1, 128),
        temporal_gain.reshape(16, 1, 128),
        jnp.transpose(spatial_qkv, (1, 0, 2)),
        spatial_out,
        spatial_up,
        spatial_down,
        jnp.transpose(temporal_qkv, (1, 0, 2)),
        temporal_out,
        temporal_up,
        temporal_down,
    )
    return result.reshape(32, 8, 128)


def solution(mesh):
    in_specs = (
        P("frame", None, "tensor"),
        P(),
        P("frame", None, "tensor"),
        P("frame", "tensor"),
        P("frame", "tensor"),
        P("frame", "tensor"),
        P(),
        P("frame", None, "tensor"),
        P("frame", "tensor"),
        P("frame", "tensor"),
        P("frame", "tensor"),
    )
    out_specs = P(None, "frame", "tensor")
    return jax.shard_map(body, mesh=mesh, in_specs=in_specs, out_specs=out_specs, check_vma=False)
```

```python
import jax
import jax.numpy as jnp
from jax import lax
from jax.experimental import pallas as pl
from jax.experimental.pallas import tpu as pltpu
from jax.sharding import PartitionSpec as P

MESH = pl.DeviceIdType.MESH
EPS = 1e-06
BF = jnp.bfloat16
F32 = jnp.float32
NT = (((1,), (1,)), ((), ()))
PARTS = 2
EACH = 8 // PARTS
ROWS = 32 * EACH
EACH_BITS, ROWS_BITS = EACH.bit_length() - 1, ROWS.bit_length() - 1
PIECES = (4, 2)

PLAN = (
    ("project", 0, 0, 2), ("first",), ("project", 0, 0, 1), ("project", 0, 0, 3), ("project", 0, 0, 0),
    ("weight", 0, False, 0), ("project", 0, 1, 2), ("sum", 0, 0, 2), ("project", 0, 1, 1), ("weight", 1, True, 1),
    ("sum", 0, 0, 1), ("project", 0, 1, 3), ("sum", 0, 0, 3), ("weight", 0, False, 1), ("project", 0, 1, 0),
    ("weight", 1, False, 0), ("sum", 0, 1, 2), ("sum", 0, 0, 0), ("sum", 0, 1, 1), ("sum", 0, 1, 3), ("turn", 0),
    ("sum", 0, 1, 0), ("weight", 0, True, 1), ("turn", 1), ("weight", 0, True, 2), ("turned", 0), ("weight", 1, False, 1),
    ("weight", 1, True, 2), ("turned", 1), ("weight", 0, False, 2), ("forward", 0, 3), ("weight", 1, False, 2),
    ("forward", 0, 2), ("forward", 0, 1), ("weight", 0, True, 3), ("weight", 0, False, 3), ("weight", 1, True, 3),
    ("weight", 1, False, 3), ("forward", 1, 3), ("weight", 0, True, 4), ("forward", 1, 2), ("forward", 1, 1),
    ("weight", 1, True, 4), ("weight", 0, False, 4), ("weight", 1, False, 4), ("enter", 0), ("project", 1, 0, 2),
    ("project", 1, 0, 1), ("project", 1, 0, 3), ("enter", 1), ("project", 1, 1, 2), ("project", 1, 1, 1), ("sum", 1, 0, 2),
    ("project", 1, 1, 3), ("sum", 1, 0, 1), ("sum", 1, 0, 3), ("sum", 1, 1, 2), ("project", 1, 0, 0), ("project", 1, 1, 0),
    ("sum", 1, 1, 1), ("sum", 1, 1, 3), ("sum", 1, 0, 0), ("sum", 1, 1, 0),
)
PLAN_FIRST = (
    ("weight", 0, True, 1), ("weight", 1, True, 1), ("weight", 0, False, 0), ("weight", 1, False, 0),
    ("weight", 2, False, 0), ("weight", 2, True, 1), ("weight", 0, True, 2), ("weight", 3, True, 1),
    ("weight", 0, False, 1), ("forward", 3), ("weight", 1, True, 2), ("weight", 1, False, 1), ("weight", 2, True, 2),
    ("weight", 3, True, 2), ("forward", 1), ("weight", 0, False, 2), ("weight", 1, False, 2), ("forward", 2),
    ("weight", 2, True, 3), ("weight", 3, True, 3), ("weight", 2, False, 2), ("weight", 2, False, 1),
    ("weight", 1, True, 3), ("weight", 1, False, 3), ("weight", 2, True, 4), ("weight", 0, False, 3),
    ("weight", 3, False, 0), ("weight", 0, True, 3), ("weight", 3, False, 1), ("weight", 3, False, 2),
    ("weight", 3, True, 4), ("weight", 3, False, 3), ("enter",), ("weight", 1, True, 4), ("weight", 1, False, 4),
    ("weight", 0, True, 4), ("weight", 2, False, 4), ("weight", 0, False, 4), ("weight", 2, False, 3),
    ("weight", 3, False, 4),
)


def norm_rows(values):
    centered = values - jnp.mean(values, axis=-1, keepdims=True)
    spread = jnp.mean(centered * centered, axis=-1, keepdims=True)
    return centered * lax.rsqrt(spread + EPS)


def kernel(
    x_in, gain1_in, gain2_in, qkv1, out1, up1, down1, qkv2, out2, up2, down2,
    y_out,
    w, gain1, gain2, x_own, xs, xt, h, terms, from_x, to_z, from_z, mid, turned, ready,
    local_sem, w_send, w_early, w_late, w_last, ag_send, ag_recv, rx_send, rx_recv, rz_send, rz_recv, turn_send, turn_recv,
):
    f, t = lax.axis_index("frame"), lax.axis_index("tensor")
    xi, zh = t // 4, t % 4
    odd, lo = f % 2, (f // 2) % 2
    f_z = (f // 4) * 4 + (f + 2) % 4
    f_core = f + 1 - 2 * odd

    def at_y(base, r):
        return (base + 4 * (r % 8)) % 32

    def tensor_at(dx, dz):
        return ((xi + dx) % 4) * 4 + (zh + dz) % 4

    def send(src, dst, send_sem, recv_sem, device):
        pltpu.make_async_remote_copy(src, dst, send_sem, recv_sem, device_id=device, device_id_type=MESH).start()

    def arrived(ref, sem):
        pltpu.make_async_remote_copy(ref, ref, sem, sem, device_id=(f_core, t), device_id_type=MESH).wait_recv()

    def left(ref, sem):
        pltpu.make_async_remote_copy(ref, ref, sem, sem, device_id=(f_core, t), device_id_type=MESH).wait_send()

    def part_order(axis):
        shapes = [(256, 1), (1, 256)]
        part = lax.broadcasted_iota(jnp.int32, shapes[axis], axis)
        own = lax.broadcasted_iota(jnp.int32, shapes[1 - axis], 1 - axis)
        natural = ((part & (ROWS - 1)) >> EACH_BITS << 3) + (part >> ROWS_BITS << EACH_BITS) + (part & (EACH - 1))
        return jnp.where(natural == own, 1.0, 0.0).astype(BF)

    barrier = pltpu.get_barrier_semaphore()
    peers = [(f_z, t), (f_core, t), (at_y(f, 1), t), (at_y(f, -1), t)]
    peers += [(f, tensor_at(dx, 0)) for dx in (1, 2, 3)] + [(f, tensor_at(0, dz)) for dz in (1, 2, 3)]
    for peer in peers:
        pl.semaphore_signal(barrier, inc=1, device_id=peer, device_id_type=MESH)
    pltpu.make_async_copy(x_in, x_own, local_sem.at[0]).start()
    pltpu.make_async_copy(gain1_in, gain1, local_sem.at[1]).start()
    pltpu.make_async_copy(gain2_in, gain2, local_sem.at[2]).start()
    for b, (qkv, up, out, down) in enumerate(((qkv1, up1, out1, down1), (qkv2, up2, out2, down2))):
        for ref, at, width in [(qkv.at[j], 128 * j, 128) for j in range(3)] + [(up, 384, 256), (out, 640, 128), (down, 768, 256)]:
            pltpu.make_async_copy(ref, w.at[b, f, :, pl.ds(at, width)], local_sem.at[3 + b]).start()

    def placed(ref, k):
        pltpu.make_async_copy(ref, ref, local_sem.at[k]).wait()

    placed(x_own, 0)
    placed(w.at[0, f], 3)
    xs[t] = jnp.dot(part_order(0), x_own[...], preferred_element_type=F32).astype(BF)
    pl.semaphore_wait(barrier, len(peers))

    used = [0, 0]

    def piece(b, i, slot):
        rows = 64 // PIECES[b]
        return w.at[b, slot, pl.ds(i * rows, rows), :]

    def w_sem(b, i, kind):
        return w_late.at[i, kind] if b else w_early.at[i, kind]

    def w_push(b, i, slot, target, kind=None):
        used[b] += 1
        send(piece(b, i, slot), piece(b, i, slot), w_send.at[b], w_last.at[b] if kind is None else w_sem(b, i, kind), (target, t))

    def w_first(b, i):
        w_push(b, i, f, f_z, 4)
        w_push(b, i, f, at_y(f, 1), 0)
        w_push(b, i, f, at_y(f, -1), 0)
        w_push(b, i, f, f_core)

    def w_rank(b, i, own, k):
        base = f if own else f_z
        early = b == 1 or i < PIECES[b] // 2
        kind = k - 1 if own else 4 + k
        rows = 64 // PIECES[b]
        both = k in (1, 2, 3)
        arrived(w.at[b, pl.ds(0, 2), pl.ds(0, rows), :] if both else piece(b, i, at_y(base, k)), w_sem(b, i, kind))
        for r in (-k, k) if both else (k,):
            slot = at_y(base, r)
            if own or early:
                if r in (-2, -1, 0):
                    w_push(b, i, slot, at_y(f, 1), kind + 1)
                if r in (0, 1, 2):
                    w_push(b, i, slot, at_y(f, -1), kind + 1)
                if early and r == (-3 if own else 3):
                    w_push(b, i, slot, at_y(f, 1 if own else -1), kind + 1)
            if own and not early:
                if r == 3:
                    w_push(b, i, at_y(f, -3 + 6 * odd), at_y(f, 1 - 2 * odd), kind + 1)
                w_push(b, i, slot, f_z, 4 + k)
            w_push(b, i, slot, f_core)

    def w_core(b):
        arrived(w.at[b, pl.ds(0, 16)], w_last.at[b])

    def gather_push(view, k, dx, dz, to_dx, to_dz):
        slot = view.at[tensor_at(4 - dx, 4 - dz)]
        send(slot, slot, ag_send.at[k], ag_recv.at[k, to_dz], (f, tensor_at(to_dx, to_dz)))

    def gather_own(view, k):
        for dz in (2, 1, 3):
            gather_push(view, k, 0, 0, 0, dz)
        for dx in (2, 1, 3):
            gather_push(view, k, 0, 0, dx, 0)

    def gather_forward(view, k, dz):
        arrived(view.at[tensor_at(0, 4 - dz)], ag_recv.at[k, dz])
        for dx in (2, 1, 3):
            gather_push(view, k, 0, dz, dx, 0)

    def gather_rest(view, k):
        arrived(view.at[pl.ds(0, 12)], ag_recv.at[k, 0])

    def normalize(view, rows, gain):
        total = view[0].astype(F32)
        for i in range(1, 16):
            total += view[i].astype(F32)
        mean = jnp.sum(total, axis=-1, keepdims=True) * (1.0 / 2048)
        square = jnp.zeros((rows, 128), F32)
        for i in range(16):
            centered = view[i].astype(F32) - mean
            square += centered * centered
        scale = lax.rsqrt(jnp.sum(square, axis=-1, keepdims=True) * (1.0 / 2048) + EPS)
        for i in range(16):
            centered = view[i].astype(F32) - mean
            h[0:rows, 128 * i : 128 * (i + 1)] = (centered * scale * gain[i]).astype(BF)

    def inner(b, rows):
        mixed = jnp.dot(h[0:rows, :], w[b, :, :, 0:640].reshape(2048, 640), preferred_element_type=F32)
        query = norm_rows(mixed[:, 0:128]).astype(BF)
        keys = norm_rows(mixed[:, 128:256]).astype(BF)
        scores = lax.dot_general(query, keys, NT, preferred_element_type=F32) * 128**-0.5
        expo = jnp.exp(scores)
        if b == 1:
            row = lax.broadcasted_iota(jnp.int32, (rows, 1), 0)
            col = lax.broadcasted_iota(jnp.int32, (1, rows), 1)
            expo = jnp.where((row & (EACH - 1)) == (col & (EACH - 1)), expo, 0.0)
        weights = (expo * (1.0 / jnp.sum(expo, axis=-1, keepdims=True))).astype(BF)
        attended = jnp.dot(weights, mixed[:, 256:384].astype(BF), preferred_element_type=F32).astype(BF)
        hidden = jax.nn.gelu(mixed[:, 384:640], approximate=True).astype(BF)
        return jnp.concatenate([attended, hidden], axis=1)

    order = (2, 1, 3, 0)

    def project(b, k, dz, both):
        for dx in (2, 1, 3, 0):
            slot = 2 * tensor_at(dx, dz)
            weight = w[b, pl.ds(slot, 2), :, 640:1024].reshape(128, 384)
            terms[b, k, dx, dz] = lax.dot_general(both, weight, NT, preferred_element_type=F32).astype(BF)
            if dx:
                send(terms.at[b, k, dx, dz], from_x.at[b, k, dz, dx - 1], rx_send.at[0], rx_recv.at[b, k, dz], (f, tensor_at(dx, 0)))

    def sum_x(b, k, dz):
        arrived(from_x.at[b, k, dz], rx_recv.at[b, k, dz])
        total = terms[b, k, 0, dz].astype(F32)
        for i in range(3):
            total += from_x[b, k, dz, i].astype(F32)
        if dz:
            to_z[b, k, dz - 1] = total.astype(BF)
            send(to_z.at[b, k, dz - 1], from_z.at[b, k, dz - 1], rz_send.at[0], rz_recv.at[b, k], (f, tensor_at(0, dz)))
        else:
            ready[b, k] = total

    def sum_z(b, k):
        arrived(from_z.at[b, k], rz_recv.at[b, k])
        total = ready[b, k]
        for i in range(3):
            total += from_z[b, k, i].astype(F32)
        return total

    distances = sorted(range(1, 32), key=lambda i: -min(i // 4, 8 - i // 4))

    def turn(k):
        middle = (xs[t, k * ROWS : (k + 1) * ROWS, :].astype(F32) + sum_z(0, k)).astype(BF).astype(F32)
        mid[k] = middle.reshape(32, EACH, 128)
        for i in distances:
            to = (f + i) % 32
            send(mid.at[k, to], turned.at[k, f], turn_send.at[k], turn_recv.at[k], (to, t))
        turned[k, f] = mid[k, f]

    def turn_done(k):
        arrived(turned.at[k, pl.ds(0, 31)], turn_recv.at[k])
        xt[k, t] = turned[k].reshape(ROWS, 128).astype(BF)

    w_first(0, 0)
    gather_own(xs, 0)
    for i in range(1, PIECES[0]):
        w_first(0, i)
    for step, *at in PLAN_FIRST:
        if step == "weight":
            w_rank(0, *at)
        elif step == "forward":
            gather_forward(xs, 0, {1: 1 + 2 * lo, 2: 2, 3: 3 - 2 * lo}[at[0]])
        elif step == "enter":
            gather_rest(xs, 0)
            placed(gain1, 1)
            normalize(xs, 256, gain1)

    w_core(0)
    branches = {}
    entered = inner(0, 256)
    for k in range(PARTS):
        branches[0, k] = entered[k * ROWS : (k + 1) * ROWS]
    placed(w.at[1, f], 4)
    placed(gain2, 2)

    for step, *at in PLAN:
        if step == "first":
            for i in range(PIECES[1]):
                w_first(1, i)
        elif step == "weight":
            w_rank(1, *at)
        elif step == "project":
            project(*at, branches[at[0], at[1]])
        elif step == "sum":
            sum_x(*at)
        elif step == "turn":
            turn(*at)
        elif step == "turned":
            turn_done(*at)
            gather_own(xt.at[at[0]], at[0] + 1)
        elif step == "forward":
            gather_forward(xt.at[at[0]], at[0] + 1, at[1])
        elif step == "enter":
            k = at[0]
            gather_rest(xt.at[k], k + 1)
            normalize(xt.at[k], ROWS, gain2)
            if k == 0:
                w_core(1)
            branches[1, k] = inner(1, ROWS)
    total = jnp.concatenate([sum_z(1, k) for k in range(PARTS)], axis=0)
    kept = jnp.concatenate([turned[k].reshape(ROWS, 128) for k in range(PARTS)], axis=0)
    y_out[...] = jnp.dot(part_order(1), (kept + total).astype(BF), preferred_element_type=F32).astype(BF)
    for b in range(2):
        left(w.at[b, pl.ds(0, used[b] // PIECES[b])], w_send.at[b])
    left(xs.at[pl.ds(0, 15)], ag_send.at[0])
    for k in range(PARTS):
        left(xt.at[k, pl.ds(0, 15)], ag_send.at[k + 1])
        left(mid.at[k, pl.ds(0, 31)], turn_send.at[k])
    left(from_x, rx_send.at[0])
    left(to_z, rz_send.at[0])


def body(
    frames_in,
    spatial_gain,
    spatial_qkv,
    spatial_out,
    spatial_up,
    spatial_down,
    temporal_gain,
    temporal_qkv,
    temporal_out,
    temporal_up,
    temporal_down,
):
    dma = pltpu.SemaphoreType.DMA
    result = pl.pallas_call(
        kernel,
        out_shape=jax.ShapeDtypeStruct((256, 128), BF),
        in_specs=[pl.BlockSpec(memory_space=pl.ANY)] * 11,
        out_specs=pl.BlockSpec(memory_space=pltpu.VMEM),
        scratch_shapes=[
            pltpu.VMEM((2, 32, 64, 1024), BF),
            pltpu.VMEM((16, 1, 128), F32),
            pltpu.VMEM((16, 1, 128), F32),
            pltpu.VMEM((256, 128), BF),
            pltpu.VMEM((16, 256, 128), BF),
            pltpu.VMEM((PARTS, 16, ROWS, 128), BF),
            pltpu.VMEM((256, 2048), BF),
            pltpu.VMEM((2, PARTS, 4, 4, ROWS, 128), BF),
            pltpu.VMEM((2, PARTS, 4, 3, ROWS, 128), BF),
            pltpu.VMEM((2, PARTS, 3, ROWS, 128), BF),
            pltpu.VMEM((2, PARTS, 3, ROWS, 128), BF),
            pltpu.VMEM((PARTS, 32, EACH, 128), F32),
            pltpu.VMEM((PARTS, 32, EACH, 128), F32),
            pltpu.VMEM((2, PARTS, ROWS, 128), F32),
            dma((5,)),
            dma((2,)),
            dma((PIECES[0], 9)),
            dma((PIECES[1], 9)),
            dma((2,)),
            dma((1 + PARTS,)),
            dma((1 + PARTS, 4)),
            dma((2,)),
            dma((2, PARTS, 4)),
            dma((1,)),
            dma((2, PARTS)),
            dma((PARTS,)),
            dma((PARTS,)),
        ],
        compiler_params=pltpu.CompilerParams(collective_id=0, has_side_effects=True, vmem_limit_bytes=63 << 20),
    )(
        frames_in.reshape(256, 128),
        spatial_gain.reshape(16, 1, 128),
        temporal_gain.reshape(16, 1, 128),
        jnp.transpose(spatial_qkv, (1, 0, 2)),
        spatial_out,
        spatial_up,
        spatial_down,
        jnp.transpose(temporal_qkv, (1, 0, 2)),
        temporal_out,
        temporal_up,
        temporal_down,
    )
    return result.reshape(32, 8, 128)


def solution(mesh):
    in_specs = (
        P("frame", None, "tensor"),
        P(),
        P("frame", None, "tensor"),
        P("frame", "tensor"),
        P("frame", "tensor"),
        P("frame", "tensor"),
        P(),
        P("frame", None, "tensor"),
        P("frame", "tensor"),
        P("frame", "tensor"),
        P("frame", "tensor"),
    )
    out_specs = P(None, "frame", "tensor")
    return jax.shard_map(body, mesh=mesh, in_specs=in_specs, out_specs=out_specs, check_vma=False)
```

```python
import jax
import jax.numpy as jnp
from jax import lax
from jax.experimental import pallas as pl
from jax.experimental.pallas import tpu as pltpu
from jax.sharding import PartitionSpec as P

MESH = pl.DeviceIdType.MESH
EPS = 1e-06
BF = jnp.bfloat16
F32 = jnp.float32
NT = (((1,), (1,)), ((), ()))
PARTS = 2
EACH = 8 // PARTS
ROWS = 32 * EACH
EACH_BITS, ROWS_BITS = EACH.bit_length() - 1, ROWS.bit_length() - 1
PIECES = (4, 2)

PLAN = (
    ("project", 0, 0, 2), ("first",), ("project", 0, 0, 1), ("project", 0, 0, 3), ("project", 0, 0, 0),
    ("weight", 0, False, 0), ("project", 0, 1, 2), ("sum", 0, 0, 2), ("project", 0, 1, 1), ("weight", 1, True, 1),
    ("sum", 0, 0, 1), ("project", 0, 1, 3), ("sum", 0, 0, 3), ("weight", 0, False, 1), ("project", 0, 1, 0),
    ("weight", 1, False, 0), ("sum", 0, 1, 2), ("sum", 0, 0, 0), ("sum", 0, 1, 1), ("sum", 0, 1, 3), ("turn", 0),
    ("sum", 0, 1, 0), ("weight", 0, True, 1), ("turn", 1), ("weight", 0, True, 2), ("turned", 0), ("weight", 1, False, 1),
    ("weight", 1, True, 2), ("turned", 1), ("weight", 0, False, 2), ("forward", 0, 3), ("weight", 1, False, 2),
    ("forward", 0, 2), ("forward", 0, 1), ("weight", 0, True, 3), ("weight", 0, False, 3), ("weight", 1, True, 3),
    ("weight", 1, False, 3), ("forward", 1, 3), ("weight", 0, True, 4), ("forward", 1, 2), ("forward", 1, 1),
    ("weight", 1, True, 4), ("weight", 0, False, 4), ("weight", 1, False, 4), ("enter", 0), ("project", 1, 0, 2),
    ("project", 1, 0, 1), ("project", 1, 0, 3), ("enter", 1), ("project", 1, 1, 2), ("project", 1, 1, 1), ("sum", 1, 0, 2),
    ("project", 1, 1, 3), ("sum", 1, 0, 1), ("sum", 1, 0, 3), ("sum", 1, 1, 2), ("project", 1, 0, 0), ("project", 1, 1, 0),
    ("sum", 1, 1, 1), ("sum", 1, 1, 3), ("sum", 1, 0, 0), ("sum", 1, 1, 0),
)


def norm_rows(values):
    centered = values - jnp.mean(values, axis=-1, keepdims=True)
    spread = jnp.mean(centered * centered, axis=-1, keepdims=True)
    return centered * lax.rsqrt(spread + EPS)


def kernel(
    x_in, gain1_in, gain2_in, qkv1, out1, up1, down1, qkv2, out2, up2, down2,
    y_out,
    w, gain1, gain2, x_own, xs, xt, h, terms, from_x, to_z, from_z, mid, turned, ready,
    local_sem, w_send, w_early, w_late, w_last, ag_send, ag_recv, rx_send, rx_recv, rz_send, rz_recv, turn_send, turn_recv,
):
    f, t = lax.axis_index("frame"), lax.axis_index("tensor")
    xi, zh = t // 4, t % 4
    odd, lo = f % 2, (f // 2) % 2
    f_z = (f // 4) * 4 + (f + 2) % 4
    f_core = f + 1 - 2 * odd

    def at_y(base, r):
        return (base + 4 * (r % 8)) % 32

    def tensor_at(dx, dz):
        return ((xi + dx) % 4) * 4 + (zh + dz) % 4

    def send(src, dst, send_sem, recv_sem, device):
        pltpu.make_async_remote_copy(src, dst, send_sem, recv_sem, device_id=device, device_id_type=MESH).start()

    def arrived(ref, sem):
        pltpu.make_async_remote_copy(ref, ref, sem, sem, device_id=(f_core, t), device_id_type=MESH).wait_recv()

    def left(ref, sem):
        pltpu.make_async_remote_copy(ref, ref, sem, sem, device_id=(f_core, t), device_id_type=MESH).wait_send()

    def part_order(axis):
        shapes = [(256, 1), (1, 256)]
        part = lax.broadcasted_iota(jnp.int32, shapes[axis], axis)
        own = lax.broadcasted_iota(jnp.int32, shapes[1 - axis], 1 - axis)
        natural = ((part & (ROWS - 1)) >> EACH_BITS << 3) + (part >> ROWS_BITS << EACH_BITS) + (part & (EACH - 1))
        return jnp.where(natural == own, 1.0, 0.0).astype(BF)

    barrier = pltpu.get_barrier_semaphore()
    peers = [(f_z, t), (f_core, t), (at_y(f, 1), t), (at_y(f, -1), t)]
    peers += [(f, tensor_at(dx, 0)) for dx in (1, 2, 3)] + [(f, tensor_at(0, dz)) for dz in (1, 2, 3)]
    for peer in peers:
        pl.semaphore_signal(barrier, inc=1, device_id=peer, device_id_type=MESH)
    pltpu.make_async_copy(x_in, x_own, local_sem.at[0]).start()
    pltpu.make_async_copy(gain1_in, gain1, local_sem.at[1]).start()
    pltpu.make_async_copy(gain2_in, gain2, local_sem.at[2]).start()
    for b, (qkv, up, out, down) in enumerate(((qkv1, up1, out1, down1), (qkv2, up2, out2, down2))):
        for ref, at, width in [(qkv.at[j], 128 * j, 128) for j in range(3)] + [(up, 384, 256), (out, 640, 128), (down, 768, 256)]:
            pltpu.make_async_copy(ref, w.at[b, f, :, pl.ds(at, width)], local_sem.at[3 + b]).start()

    def placed(ref, k):
        pltpu.make_async_copy(ref, ref, local_sem.at[k]).wait()

    placed(x_own, 0)
    placed(w.at[0, f], 3)
    xs[t] = jnp.dot(part_order(0), x_own[...], preferred_element_type=F32).astype(BF)
    pl.semaphore_wait(barrier, len(peers))

    used = [0, 0]

    def piece(b, i, slot):
        rows = 64 // PIECES[b]
        return w.at[b, slot, pl.ds(i * rows, rows), :]

    def w_sem(b, i, kind):
        return w_late.at[i, kind] if b else w_early.at[i, kind]

    def w_push(b, i, slot, target, kind=None):
        used[b] += 1
        send(piece(b, i, slot), piece(b, i, slot), w_send.at[b], w_last.at[b] if kind is None else w_sem(b, i, kind), (target, t))

    def w_first(b, i):
        w_push(b, i, f, f_z, 4)
        w_push(b, i, f, at_y(f, 1), 0)
        w_push(b, i, f, at_y(f, -1), 0)
        w_push(b, i, f, f_core)

    def w_rank(b, i, own, k):
        base = f if own else f_z
        early = b == 1 or i < PIECES[b] // 2
        kind = k - 1 if own else 4 + k
        rows = 64 // PIECES[b]
        both = k in (1, 2, 3)
        arrived(w.at[b, pl.ds(0, 2), pl.ds(0, rows), :] if both else piece(b, i, at_y(base, k)), w_sem(b, i, kind))
        for r in (-k, k) if both else (k,):
            slot = at_y(base, r)
            if own or early:
                if r in (-2, -1, 0):
                    w_push(b, i, slot, at_y(f, 1), kind + 1)
                if r in (0, 1, 2):
                    w_push(b, i, slot, at_y(f, -1), kind + 1)
                if early and r == (-3 if own else 3):
                    w_push(b, i, slot, at_y(f, 1 if own else -1), kind + 1)
            if own and not early:
                if r == 3:
                    w_push(b, i, at_y(f, -3 + 6 * odd), at_y(f, 1 - 2 * odd), kind + 1)
                w_push(b, i, slot, f_z, 4 + k)
            w_push(b, i, slot, f_core)

    def w_core(b):
        arrived(w.at[b, pl.ds(0, 16)], w_last.at[b])

    def gather_push(view, k, dx, dz, to_dx, to_dz):
        slot = view.at[tensor_at(4 - dx, 4 - dz)]
        send(slot, slot, ag_send.at[k], ag_recv.at[k, to_dz], (f, tensor_at(to_dx, to_dz)))

    def gather_own(view, k):
        for dz in (1, 3, 2):
            gather_push(view, k, 0, 0, 0, dz)
        for dx in (2, 1, 3):
            gather_push(view, k, 0, 0, dx, 0)

    def gather_forward(view, k, dz):
        arrived(view.at[tensor_at(0, 4 - dz)], ag_recv.at[k, dz])
        for dx in (2, 1, 3):
            gather_push(view, k, 0, dz, dx, 0)

    def gather_rest(view, k):
        arrived(view.at[pl.ds(0, 12)], ag_recv.at[k, 0])

    def normalize(view, rows, gain):
        total = view[0].astype(F32)
        for i in range(1, 16):
            total += view[i].astype(F32)
        mean = jnp.sum(total, axis=-1, keepdims=True) * (1.0 / 2048)
        square = jnp.zeros((rows, 128), F32)
        for i in range(16):
            centered = view[i].astype(F32) - mean
            square += centered * centered
        scale = lax.rsqrt(jnp.sum(square, axis=-1, keepdims=True) * (1.0 / 2048) + EPS)
        for i in range(16):
            centered = view[i].astype(F32) - mean
            h[0:rows, 128 * i : 128 * (i + 1)] = (centered * scale * gain[i]).astype(BF)

    def inner(b, rows):
        mixed = jnp.dot(h[0:rows, :], w[b, :, :, 0:640].reshape(2048, 640), preferred_element_type=F32)
        query = norm_rows(mixed[:, 0:128]).astype(BF)
        keys = norm_rows(mixed[:, 128:256]).astype(BF)
        scores = lax.dot_general(query, keys, NT, preferred_element_type=F32) * 128**-0.5
        expo = jnp.exp(scores)
        if b == 1:
            row = lax.broadcasted_iota(jnp.int32, (rows, 1), 0)
            col = lax.broadcasted_iota(jnp.int32, (1, rows), 1)
            expo = jnp.where((row & (EACH - 1)) == (col & (EACH - 1)), expo, 0.0)
        weights = (expo * (1.0 / jnp.sum(expo, axis=-1, keepdims=True))).astype(BF)
        attended = jnp.dot(weights, mixed[:, 256:384].astype(BF), preferred_element_type=F32).astype(BF)
        hidden = jax.nn.gelu(mixed[:, 384:640], approximate=True).astype(BF)
        return jnp.concatenate([attended, hidden], axis=1)

    order = (2, 1, 3, 0)

    def project(b, k, dz, both):
        for dx in (2, 1, 3, 0):
            slot = 2 * tensor_at(dx, dz)
            weight = w[b, pl.ds(slot, 2), :, 640:1024].reshape(128, 384)
            terms[b, k, dx, dz] = lax.dot_general(both, weight, NT, preferred_element_type=F32).astype(BF)
            if dx:
                send(terms.at[b, k, dx, dz], from_x.at[b, k, dz, dx - 1], rx_send.at[0], rx_recv.at[b, k, dz], (f, tensor_at(dx, 0)))

    def sum_x(b, k, dz):
        arrived(from_x.at[b, k, dz], rx_recv.at[b, k, dz])
        total = terms[b, k, 0, dz].astype(F32)
        for i in range(3):
            total += from_x[b, k, dz, i].astype(F32)
        if dz:
            to_z[b, k, dz - 1] = total.astype(BF)
            send(to_z.at[b, k, dz - 1], from_z.at[b, k, dz - 1], rz_send.at[0], rz_recv.at[b, k], (f, tensor_at(0, dz)))
        else:
            ready[b, k] = total

    def sum_z(b, k):
        arrived(from_z.at[b, k], rz_recv.at[b, k])
        total = ready[b, k]
        for i in range(3):
            total += from_z[b, k, i].astype(F32)
        return total

    distances = sorted(range(1, 32), key=lambda i: -min(i // 4, 8 - i // 4))

    def turn(k):
        middle = (xs[t, k * ROWS : (k + 1) * ROWS, :].astype(F32) + sum_z(0, k)).astype(BF).astype(F32)
        mid[k] = middle.reshape(32, EACH, 128)
        for i in distances:
            to = (f + i) % 32
            send(mid.at[k, to], turned.at[k, f], turn_send.at[k], turn_recv.at[k], (to, t))
        turned[k, f] = mid[k, f]

    def turn_done(k):
        arrived(turned.at[k, pl.ds(0, 31)], turn_recv.at[k])
        xt[k, t] = turned[k].reshape(ROWS, 128).astype(BF)

    pieces = range(PIECES[0])
    early, late = pieces[: PIECES[0] // 2], pieces[PIECES[0] // 2 :]
    for i in pieces:
        w_first(0, i)
    gather_own(xs, 0)
    for i in pieces:
        w_rank(0, i, True, 1)
    for i in pieces:
        w_rank(0, i, False, 0)
    for i in early:
        w_rank(0, i, True, 2)
    gather_forward(xs, 0, 3 - 2 * lo)
    for i in late:
        w_rank(0, i, True, 2)
    for i in pieces:
        w_rank(0, i, False, 1)
    for i in early:
        w_rank(0, i, True, 3)
    gather_forward(xs, 0, 1 + 2 * lo)
    for i in late:
        w_rank(0, i, True, 3)
    gather_forward(xs, 0, 2)
    for i in (*late, *early):
        w_rank(0, i, False, 2)
    for i in pieces:
        w_rank(0, i, True, 4)
    for i in (*late, *early):
        w_rank(0, i, False, 3)
    for i in late:
        w_rank(0, i, False, 4)
    gather_rest(xs, 0)
    placed(gain1, 1)
    normalize(xs, 256, gain1)
    for i in early:
        w_rank(0, i, False, 4)

    w_core(0)
    branches = {}
    entered = inner(0, 256)
    for k in range(PARTS):
        branches[0, k] = entered[k * ROWS : (k + 1) * ROWS]
    placed(w.at[1, f], 4)
    placed(gain2, 2)

    for step, *at in PLAN:
        if step == "first":
            for i in range(PIECES[1]):
                w_first(1, i)
        elif step == "weight":
            w_rank(1, *at)
        elif step == "project":
            project(*at, branches[at[0], at[1]])
        elif step == "sum":
            sum_x(*at)
        elif step == "turn":
            turn(*at)
        elif step == "turned":
            turn_done(*at)
            gather_own(xt.at[at[0]], at[0] + 1)
        elif step == "forward":
            gather_forward(xt.at[at[0]], at[0] + 1, at[1])
        elif step == "enter":
            k = at[0]
            gather_rest(xt.at[k], k + 1)
            normalize(xt.at[k], ROWS, gain2)
            if k == 0:
                w_core(1)
            branches[1, k] = inner(1, ROWS)
    total = jnp.concatenate([sum_z(1, k) for k in range(PARTS)], axis=0)
    kept = jnp.concatenate([turned[k].reshape(ROWS, 128) for k in range(PARTS)], axis=0)
    y_out[...] = jnp.dot(part_order(1), (kept + total).astype(BF), preferred_element_type=F32).astype(BF)
    for b in range(2):
        left(w.at[b, pl.ds(0, used[b] // PIECES[b])], w_send.at[b])
    left(xs.at[pl.ds(0, 15)], ag_send.at[0])
    for k in range(PARTS):
        left(xt.at[k, pl.ds(0, 15)], ag_send.at[k + 1])
        left(mid.at[k, pl.ds(0, 31)], turn_send.at[k])
    left(from_x, rx_send.at[0])
    left(to_z, rz_send.at[0])


def body(
    frames_in,
    spatial_gain,
    spatial_qkv,
    spatial_out,
    spatial_up,
    spatial_down,
    temporal_gain,
    temporal_qkv,
    temporal_out,
    temporal_up,
    temporal_down,
):
    dma = pltpu.SemaphoreType.DMA
    result = pl.pallas_call(
        kernel,
        out_shape=jax.ShapeDtypeStruct((256, 128), BF),
        in_specs=[pl.BlockSpec(memory_space=pl.ANY)] * 11,
        out_specs=pl.BlockSpec(memory_space=pltpu.VMEM),
        scratch_shapes=[
            pltpu.VMEM((2, 32, 64, 1024), BF),
            pltpu.VMEM((16, 1, 128), F32),
            pltpu.VMEM((16, 1, 128), F32),
            pltpu.VMEM((256, 128), BF),
            pltpu.VMEM((16, 256, 128), BF),
            pltpu.VMEM((PARTS, 16, ROWS, 128), BF),
            pltpu.VMEM((256, 2048), BF),
            pltpu.VMEM((2, PARTS, 4, 4, ROWS, 128), BF),
            pltpu.VMEM((2, PARTS, 4, 3, ROWS, 128), BF),
            pltpu.VMEM((2, PARTS, 3, ROWS, 128), BF),
            pltpu.VMEM((2, PARTS, 3, ROWS, 128), BF),
            pltpu.VMEM((PARTS, 32, EACH, 128), F32),
            pltpu.VMEM((PARTS, 32, EACH, 128), F32),
            pltpu.VMEM((2, PARTS, ROWS, 128), F32),
            dma((5,)),
            dma((2,)),
            dma((PIECES[0], 9)),
            dma((PIECES[1], 9)),
            dma((2,)),
            dma((1 + PARTS,)),
            dma((1 + PARTS, 4)),
            dma((2,)),
            dma((2, PARTS, 4)),
            dma((1,)),
            dma((2, PARTS)),
            dma((PARTS,)),
            dma((PARTS,)),
        ],
        compiler_params=pltpu.CompilerParams(collective_id=0, has_side_effects=True, vmem_limit_bytes=63 << 20),
    )(
        frames_in.reshape(256, 128),
        spatial_gain.reshape(16, 1, 128),
        temporal_gain.reshape(16, 1, 128),
        jnp.transpose(spatial_qkv, (1, 0, 2)),
        spatial_out,
        spatial_up,
        spatial_down,
        jnp.transpose(temporal_qkv, (1, 0, 2)),
        temporal_out,
        temporal_up,
        temporal_down,
    )
    return result.reshape(32, 8, 128)


def solution(mesh):
    in_specs = (
        P("frame", None, "tensor"),
        P(),
        P("frame", None, "tensor"),
        P("frame", "tensor"),
        P("frame", "tensor"),
        P("frame", "tensor"),
        P(),
        P("frame", None, "tensor"),
        P("frame", "tensor"),
        P("frame", "tensor"),
        P("frame", "tensor"),
    )
    out_specs = P(None, "frame", "tensor")
    return jax.shard_map(body, mesh=mesh, in_specs=in_specs, out_specs=out_specs, check_vma=False)
```

```python
import jax
import jax.numpy as jnp
from jax import lax
from jax.experimental import pallas as pl
from jax.experimental.pallas import tpu as pltpu
from jax.sharding import PartitionSpec as P

MESH = pl.DeviceIdType.MESH
EPS = 1e-06
BF = jnp.bfloat16
F32 = jnp.float32
NT = (((1,), (1,)), ((), ()))
PARTS = 2
EACH = 8 // PARTS
ROWS = 32 * EACH
EACH_BITS, ROWS_BITS = EACH.bit_length() - 1, ROWS.bit_length() - 1
PIECES = (4, 2)

PLAN = (
    ("first",), ("project", 0, 0, 2), ("project", 0, 0, 1), ("project", 0, 0, 3), ("project", 0, 0, 0),
    ("weight", 0, False, 0), ("project", 0, 1, 2), ("sum", 0, 0, 2), ("project", 0, 1, 1), ("weight", 1, True, 1),
    ("sum", 0, 0, 1), ("project", 0, 1, 3), ("sum", 0, 0, 3), ("weight", 0, False, 1), ("project", 0, 1, 0),
    ("weight", 1, False, 0), ("sum", 0, 1, 2), ("sum", 0, 0, 0), ("sum", 0, 1, 1), ("sum", 0, 1, 3), ("turn", 0),
    ("sum", 0, 1, 0), ("weight", 0, True, 1), ("turn", 1), ("weight", 0, True, 2), ("turned", 0), ("weight", 1, False, 1),
    ("weight", 1, True, 2), ("turned", 1), ("weight", 0, False, 2), ("forward", 0, 3), ("weight", 1, False, 2),
    ("forward", 0, 2), ("forward", 0, 1), ("weight", 0, True, 3), ("weight", 0, False, 3), ("weight", 1, True, 3),
    ("weight", 1, False, 3), ("forward", 1, 3), ("weight", 0, True, 4), ("forward", 1, 2), ("forward", 1, 1),
    ("weight", 1, True, 4), ("weight", 0, False, 4), ("weight", 1, False, 4), ("enter", 0), ("project", 1, 0, 2),
    ("project", 1, 0, 1), ("project", 1, 0, 3), ("enter", 1), ("project", 1, 1, 2), ("project", 1, 1, 1), ("sum", 1, 0, 2),
    ("project", 1, 1, 3), ("sum", 1, 0, 1), ("sum", 1, 0, 3), ("sum", 1, 1, 2), ("project", 1, 0, 0), ("project", 1, 1, 0),
    ("sum", 1, 1, 1), ("sum", 1, 1, 3), ("sum", 1, 0, 0), ("sum", 1, 1, 0),
)


def norm_rows(values):
    centered = values - jnp.mean(values, axis=-1, keepdims=True)
    spread = jnp.mean(centered * centered, axis=-1, keepdims=True)
    return centered * lax.rsqrt(spread + EPS)


def kernel(
    x_in, gain1_in, gain2_in, qkv1, out1, up1, down1, qkv2, out2, up2, down2,
    y_out,
    w, gain1, gain2, x_own, xs, xt, h, terms, from_x, to_z, from_z, mid, turned, ready,
    local_sem, w_send, w_early, w_late, w_last, ag_send, ag_recv, rx_send, rx_recv, rz_send, rz_recv, turn_send, turn_recv,
):
    f, t = lax.axis_index("frame"), lax.axis_index("tensor")
    xi, zh = t // 4, t % 4
    odd, lo = f % 2, (f // 2) % 2
    f_z = (f // 4) * 4 + (f + 2) % 4
    f_core = f + 1 - 2 * odd

    def at_y(base, r):
        return (base + 4 * (r % 8)) % 32

    def tensor_at(dx, dz):
        return ((xi + dx) % 4) * 4 + (zh + dz) % 4

    def send(src, dst, send_sem, recv_sem, device):
        pltpu.make_async_remote_copy(src, dst, send_sem, recv_sem, device_id=device, device_id_type=MESH).start()

    def arrived(ref, sem):
        pltpu.make_async_remote_copy(ref, ref, sem, sem, device_id=(f_core, t), device_id_type=MESH).wait_recv()

    def left(ref, sem):
        pltpu.make_async_remote_copy(ref, ref, sem, sem, device_id=(f_core, t), device_id_type=MESH).wait_send()

    def part_order(axis):
        shapes = [(256, 1), (1, 256)]
        part = lax.broadcasted_iota(jnp.int32, shapes[axis], axis)
        own = lax.broadcasted_iota(jnp.int32, shapes[1 - axis], 1 - axis)
        natural = ((part & (ROWS - 1)) >> EACH_BITS << 3) + (part >> ROWS_BITS << EACH_BITS) + (part & (EACH - 1))
        return jnp.where(natural == own, 1.0, 0.0).astype(BF)

    barrier = pltpu.get_barrier_semaphore()
    peers = [(f_z, t), (f_core, t), (at_y(f, 1), t), (at_y(f, -1), t)]
    peers += [(f, tensor_at(dx, 0)) for dx in (1, 2, 3)] + [(f, tensor_at(0, dz)) for dz in (1, 2, 3)]
    for peer in peers:
        pl.semaphore_signal(barrier, inc=1, device_id=peer, device_id_type=MESH)
    pltpu.make_async_copy(x_in, x_own, local_sem.at[0]).start()
    pltpu.make_async_copy(gain1_in, gain1, local_sem.at[1]).start()
    pltpu.make_async_copy(gain2_in, gain2, local_sem.at[2]).start()
    for b, (qkv, up, out, down) in enumerate(((qkv1, up1, out1, down1), (qkv2, up2, out2, down2))):
        for ref, at, width in [(qkv.at[j], 128 * j, 128) for j in range(3)] + [(up, 384, 256), (out, 640, 128), (down, 768, 256)]:
            pltpu.make_async_copy(ref, w.at[b, f, :, pl.ds(at, width)], local_sem.at[3 + b]).start()

    def placed(ref, k):
        pltpu.make_async_copy(ref, ref, local_sem.at[k]).wait()

    placed(x_own, 0)
    placed(w.at[0, f], 3)
    xs[t] = jnp.dot(part_order(0), x_own[...], preferred_element_type=F32).astype(BF)
    pl.semaphore_wait(barrier, len(peers))

    used = [0, 0]

    def piece(b, i, slot):
        rows = 64 // PIECES[b]
        return w.at[b, slot, pl.ds(i * rows, rows), :]

    def w_sem(b, i, kind):
        return w_late.at[i, kind] if b else w_early.at[i, kind]

    def w_push(b, i, slot, target, kind=None):
        used[b] += 1
        send(piece(b, i, slot), piece(b, i, slot), w_send.at[b], w_last.at[b] if kind is None else w_sem(b, i, kind), (target, t))

    def w_first(b, i):
        w_push(b, i, f, f_z, 4)
        w_push(b, i, f, at_y(f, 1), 0)
        w_push(b, i, f, at_y(f, -1), 0)
        w_push(b, i, f, f_core)

    def w_rank(b, i, own, k):
        base = f if own else f_z
        early = b == 1 or i < PIECES[b] // 2
        kind = k - 1 if own else 4 + k
        rows = 64 // PIECES[b]
        both = k in (1, 2, 3)
        arrived(w.at[b, pl.ds(0, 2), pl.ds(0, rows), :] if both else piece(b, i, at_y(base, k)), w_sem(b, i, kind))
        for r in (-k, k) if both else (k,):
            slot = at_y(base, r)
            if own or early:
                if r in (-2, -1, 0):
                    w_push(b, i, slot, at_y(f, 1), kind + 1)
                if r in (0, 1, 2):
                    w_push(b, i, slot, at_y(f, -1), kind + 1)
                if early and r == (-3 if own else 3):
                    w_push(b, i, slot, at_y(f, 1 if own else -1), kind + 1)
            if own and not early:
                if r == 3:
                    w_push(b, i, at_y(f, -3 + 6 * odd), at_y(f, 1 - 2 * odd), kind + 1)
                w_push(b, i, slot, f_z, 4 + k)
            w_push(b, i, slot, f_core)

    def w_core(b):
        arrived(w.at[b, pl.ds(0, 16)], w_last.at[b])

    def gather_push(view, k, dx, dz, to_dx, to_dz):
        slot = view.at[tensor_at(4 - dx, 4 - dz)]
        send(slot, slot, ag_send.at[k], ag_recv.at[k, to_dz], (f, tensor_at(to_dx, to_dz)))

    def gather_own(view, k):
        for dz in (1, 3, 2):
            gather_push(view, k, 0, 0, 0, dz)
        for dx in (2, 1, 3):
            gather_push(view, k, 0, 0, dx, 0)

    def gather_forward(view, k, dz):
        arrived(view.at[tensor_at(0, 4 - dz)], ag_recv.at[k, dz])
        for dx in (2, 1, 3):
            gather_push(view, k, 0, dz, dx, 0)

    def gather_rest(view, k):
        arrived(view.at[pl.ds(0, 12)], ag_recv.at[k, 0])

    def normalize(view, rows, gain):
        total = view[0].astype(F32)
        for i in range(1, 16):
            total += view[i].astype(F32)
        mean = jnp.sum(total, axis=-1, keepdims=True) * (1.0 / 2048)
        square = jnp.zeros((rows, 128), F32)
        for i in range(16):
            centered = view[i].astype(F32) - mean
            square += centered * centered
        scale = lax.rsqrt(jnp.sum(square, axis=-1, keepdims=True) * (1.0 / 2048) + EPS)
        for i in range(16):
            centered = view[i].astype(F32) - mean
            h[0:rows, 128 * i : 128 * (i + 1)] = (centered * scale * gain[i]).astype(BF)

    def inner(b, rows):
        mixed = jnp.dot(h[0:rows, :], w[b, :, :, 0:640].reshape(2048, 640), preferred_element_type=F32)
        query = norm_rows(mixed[:, 0:128]).astype(BF)
        keys = norm_rows(mixed[:, 128:256]).astype(BF)
        scores = lax.dot_general(query, keys, NT, preferred_element_type=F32) * 128**-0.5
        expo = jnp.exp(scores)
        if b == 1:
            row = lax.broadcasted_iota(jnp.int32, (rows, 1), 0)
            col = lax.broadcasted_iota(jnp.int32, (1, rows), 1)
            expo = jnp.where((row & (EACH - 1)) == (col & (EACH - 1)), expo, 0.0)
        weights = (expo * (1.0 / jnp.sum(expo, axis=-1, keepdims=True))).astype(BF)
        attended = jnp.dot(weights, mixed[:, 256:384].astype(BF), preferred_element_type=F32).astype(BF)
        hidden = jax.nn.gelu(mixed[:, 384:640], approximate=True).astype(BF)
        return jnp.concatenate([attended, hidden], axis=1)

    order = (2, 1, 3, 0)

    def project(b, k, dz, both):
        for pair in ((2, 1), (3, 0)):
            weight = [w[b, pl.ds(2 * tensor_at(dx, dz), 2), :, 640:1024].reshape(128, 384) for dx in pair]
            product = lax.dot_general(both, jnp.concatenate(weight, axis=0), NT, preferred_element_type=F32).astype(BF)
            for n, dx in enumerate(pair):
                terms[b, k, dx, dz] = product[:, 128 * n : 128 * (n + 1)]
                if dx:
                    send(terms.at[b, k, dx, dz], from_x.at[b, k, dz, dx - 1], rx_send.at[0], rx_recv.at[b, k, dz], (f, tensor_at(dx, 0)))

    def sum_x(b, k, dz):
        arrived(from_x.at[b, k, dz], rx_recv.at[b, k, dz])
        total = terms[b, k, 0, dz].astype(F32)
        for i in range(3):
            total += from_x[b, k, dz, i].astype(F32)
        if dz:
            to_z[b, k, dz - 1] = total.astype(BF)
            send(to_z.at[b, k, dz - 1], from_z.at[b, k, dz - 1], rz_send.at[0], rz_recv.at[b, k], (f, tensor_at(0, dz)))
        else:
            ready[b, k] = total

    def sum_z(b, k):
        arrived(from_z.at[b, k], rz_recv.at[b, k])
        total = ready[b, k]
        for i in range(3):
            total += from_z[b, k, i].astype(F32)
        return total

    distances = sorted(range(1, 32), key=lambda i: -min(i // 4, 8 - i // 4))

    def turn(k):
        middle = (xs[t, k * ROWS : (k + 1) * ROWS, :].astype(F32) + sum_z(0, k)).astype(BF).astype(F32)
        mid[k] = middle.reshape(32, EACH, 128)
        for i in distances:
            to = (f + i) % 32
            send(mid.at[k, to], turned.at[k, f], turn_send.at[k], turn_recv.at[k], (to, t))
        turned[k, f] = mid[k, f]

    def turn_done(k):
        arrived(turned.at[k, pl.ds(0, 31)], turn_recv.at[k])
        xt[k, t] = turned[k].reshape(ROWS, 128).astype(BF)

    pieces = range(PIECES[0])
    early, late = pieces[: PIECES[0] // 2], pieces[PIECES[0] // 2 :]
    for i in pieces:
        w_first(0, i)
    gather_own(xs, 0)
    for i in pieces:
        w_rank(0, i, True, 1)
    for i in pieces:
        w_rank(0, i, False, 0)
    for i in early:
        w_rank(0, i, True, 2)
    gather_forward(xs, 0, 3 - 2 * lo)
    for i in late:
        w_rank(0, i, True, 2)
    for i in pieces:
        w_rank(0, i, False, 1)
    for i in early:
        w_rank(0, i, True, 3)
    gather_forward(xs, 0, 1 + 2 * lo)
    for i in late:
        w_rank(0, i, True, 3)
    gather_forward(xs, 0, 2)
    for i in (*late, *early):
        w_rank(0, i, False, 2)
    for i in pieces:
        w_rank(0, i, True, 4)
    for i in (*late, *early):
        w_rank(0, i, False, 3)
    for i in late:
        w_rank(0, i, False, 4)
    gather_rest(xs, 0)
    placed(gain1, 1)
    normalize(xs, 256, gain1)
    for i in early:
        w_rank(0, i, False, 4)

    w_core(0)
    branches = {}
    entered = inner(0, 256)
    for k in range(PARTS):
        branches[0, k] = entered[k * ROWS : (k + 1) * ROWS]
    placed(w.at[1, f], 4)
    placed(gain2, 2)

    for step, *at in PLAN:
        if step == "first":
            for i in range(PIECES[1]):
                w_first(1, i)
        elif step == "weight":
            w_rank(1, *at)
        elif step == "project":
            project(*at, branches[at[0], at[1]])
        elif step == "sum":
            sum_x(*at)
        elif step == "turn":
            turn(*at)
        elif step == "turned":
            turn_done(*at)
            gather_own(xt.at[at[0]], at[0] + 1)
        elif step == "forward":
            gather_forward(xt.at[at[0]], at[0] + 1, at[1])
        elif step == "enter":
            k = at[0]
            gather_rest(xt.at[k], k + 1)
            normalize(xt.at[k], ROWS, gain2)
            if k == 0:
                w_core(1)
            branches[1, k] = inner(1, ROWS)
    total = jnp.concatenate([sum_z(1, k) for k in range(PARTS)], axis=0)
    kept = jnp.concatenate([turned[k].reshape(ROWS, 128) for k in range(PARTS)], axis=0)
    y_out[...] = jnp.dot(part_order(1), (kept + total).astype(BF), preferred_element_type=F32).astype(BF)
    for b in range(2):
        left(w.at[b, pl.ds(0, used[b] // PIECES[b])], w_send.at[b])
    left(xs.at[pl.ds(0, 15)], ag_send.at[0])
    for k in range(PARTS):
        left(xt.at[k, pl.ds(0, 15)], ag_send.at[k + 1])
        left(mid.at[k, pl.ds(0, 31)], turn_send.at[k])
    left(from_x, rx_send.at[0])
    left(to_z, rz_send.at[0])


def body(
    frames_in,
    spatial_gain,
    spatial_qkv,
    spatial_out,
    spatial_up,
    spatial_down,
    temporal_gain,
    temporal_qkv,
    temporal_out,
    temporal_up,
    temporal_down,
):
    dma = pltpu.SemaphoreType.DMA
    result = pl.pallas_call(
        kernel,
        out_shape=jax.ShapeDtypeStruct((256, 128), BF),
        in_specs=[pl.BlockSpec(memory_space=pl.ANY)] * 11,
        out_specs=pl.BlockSpec(memory_space=pltpu.VMEM),
        scratch_shapes=[
            pltpu.VMEM((2, 32, 64, 1024), BF),
            pltpu.VMEM((16, 1, 128), F32),
            pltpu.VMEM((16, 1, 128), F32),
            pltpu.VMEM((256, 128), BF),
            pltpu.VMEM((16, 256, 128), BF),
            pltpu.VMEM((PARTS, 16, ROWS, 128), BF),
            pltpu.VMEM((256, 2048), BF),
            pltpu.VMEM((2, PARTS, 4, 4, ROWS, 128), BF),
            pltpu.VMEM((2, PARTS, 4, 3, ROWS, 128), BF),
            pltpu.VMEM((2, PARTS, 3, ROWS, 128), BF),
            pltpu.VMEM((2, PARTS, 3, ROWS, 128), BF),
            pltpu.VMEM((PARTS, 32, EACH, 128), F32),
            pltpu.VMEM((PARTS, 32, EACH, 128), F32),
            pltpu.VMEM((2, PARTS, ROWS, 128), F32),
            dma((5,)),
            dma((2,)),
            dma((PIECES[0], 9)),
            dma((PIECES[1], 9)),
            dma((2,)),
            dma((1 + PARTS,)),
            dma((1 + PARTS, 4)),
            dma((2,)),
            dma((2, PARTS, 4)),
            dma((1,)),
            dma((2, PARTS)),
            dma((PARTS,)),
            dma((PARTS,)),
        ],
        compiler_params=pltpu.CompilerParams(collective_id=0, has_side_effects=True, vmem_limit_bytes=63 << 20),
    )(
        frames_in.reshape(256, 128),
        spatial_gain.reshape(16, 1, 128),
        temporal_gain.reshape(16, 1, 128),
        jnp.transpose(spatial_qkv, (1, 0, 2)),
        spatial_out,
        spatial_up,
        spatial_down,
        jnp.transpose(temporal_qkv, (1, 0, 2)),
        temporal_out,
        temporal_up,
        temporal_down,
    )
    return result.reshape(32, 8, 128)


def solution(mesh):
    in_specs = (
        P("frame", None, "tensor"),
        P(),
        P("frame", None, "tensor"),
        P("frame", "tensor"),
        P("frame", "tensor"),
        P("frame", "tensor"),
        P(),
        P("frame", None, "tensor"),
        P("frame", "tensor"),
        P("frame", "tensor"),
        P("frame", "tensor"),
    )
    out_specs = P(None, "frame", "tensor")
    return jax.shard_map(body, mesh=mesh, in_specs=in_specs, out_specs=out_specs, check_vma=False)
```

```python
import jax
import jax.numpy as jnp
from jax import lax
from jax.experimental import pallas as pl
from jax.experimental.pallas import tpu as pltpu
from jax.sharding import PartitionSpec as P

MESH = pl.DeviceIdType.MESH
EPS = 1e-06
BF = jnp.bfloat16
F32 = jnp.float32
NT = (((1,), (1,)), ((), ()))
PARTS = 2
EACH = 8 // PARTS
ROWS = 32 * EACH
EACH_BITS, ROWS_BITS = EACH.bit_length() - 1, ROWS.bit_length() - 1
PIECES = (4, 2)

PLAN = (
    ("first",), ("project", 0, 0, 2), ("project", 0, 0, 1), ("project", 0, 0, 3), ("project", 0, 0, 0),
    ("weight", 0, False, 0), ("project", 0, 1, 2), ("sum", 0, 0, 2), ("project", 0, 1, 1), ("weight", 1, True, 1),
    ("sum", 0, 0, 1), ("project", 0, 1, 3), ("sum", 0, 0, 3), ("weight", 0, False, 1), ("project", 0, 1, 0),
    ("weight", 1, False, 0), ("sum", 0, 1, 2), ("sum", 0, 0, 0), ("sum", 0, 1, 1), ("sum", 0, 1, 3), ("turn", 0),
    ("sum", 0, 1, 0), ("weight", 0, True, 1), ("turn", 1), ("weight", 0, True, 2), ("turned", 0), ("weight", 1, False, 1),
    ("weight", 1, True, 2), ("turned", 1), ("weight", 0, False, 2), ("forward", 0, 3), ("weight", 1, False, 2),
    ("forward", 0, 2), ("forward", 0, 1), ("weight", 0, True, 3), ("weight", 0, False, 3), ("weight", 1, True, 3),
    ("weight", 1, False, 3), ("forward", 1, 3), ("weight", 0, True, 4), ("forward", 1, 2), ("forward", 1, 1),
    ("weight", 1, True, 4), ("weight", 0, False, 4), ("weight", 1, False, 4), ("enter", 0), ("project", 1, 0, 2),
    ("project", 1, 0, 1), ("project", 1, 0, 3), ("enter", 1), ("project", 1, 1, 2), ("project", 1, 1, 1), ("sum", 1, 0, 2),
    ("project", 1, 1, 3), ("sum", 1, 0, 1), ("sum", 1, 0, 3), ("sum", 1, 1, 2), ("project", 1, 0, 0), ("project", 1, 1, 0),
    ("sum", 1, 1, 1), ("sum", 1, 1, 3), ("sum", 1, 0, 0), ("sum", 1, 1, 0),
)


def norm_rows(values):
    centered = values - jnp.mean(values, axis=-1, keepdims=True)
    spread = jnp.mean(centered * centered, axis=-1, keepdims=True)
    return centered * lax.rsqrt(spread + EPS)


def kernel(
    x_in, gain1_in, gain2_in, qkv1, out1, up1, down1, qkv2, out2, up2, down2,
    y_out,
    w, gain1, gain2, x_own, xs, xt, h, terms, from_x, to_z, from_z, mid, turned, ready,
    local_sem, w_send, w_early, w_late, w_last, ag_send, ag_recv, rx_send, rx_recv, rz_send, rz_recv, turn_send, turn_recv,
):
    f, t = lax.axis_index("frame"), lax.axis_index("tensor")
    xi, zh = t // 4, t % 4
    odd, lo = f % 2, (f // 2) % 2
    f_z = (f // 4) * 4 + (f + 2) % 4
    f_core = f + 1 - 2 * odd

    def at_y(base, r):
        return (base + 4 * (r % 8)) % 32

    def tensor_at(dx, dz):
        return ((xi + dx) % 4) * 4 + (zh + dz) % 4

    def send(src, dst, send_sem, recv_sem, device):
        pltpu.make_async_remote_copy(src, dst, send_sem, recv_sem, device_id=device, device_id_type=MESH).start()

    def arrived(ref, sem):
        pltpu.make_async_remote_copy(ref, ref, sem, sem, device_id=(f_core, t), device_id_type=MESH).wait_recv()

    def left(ref, sem):
        pltpu.make_async_remote_copy(ref, ref, sem, sem, device_id=(f_core, t), device_id_type=MESH).wait_send()

    def part_order(axis):
        shapes = [(256, 1), (1, 256)]
        part = lax.broadcasted_iota(jnp.int32, shapes[axis], axis)
        own = lax.broadcasted_iota(jnp.int32, shapes[1 - axis], 1 - axis)
        natural = ((part & (ROWS - 1)) >> EACH_BITS << 3) + (part >> ROWS_BITS << EACH_BITS) + (part & (EACH - 1))
        return jnp.where(natural == own, 1.0, 0.0).astype(BF)

    barrier = pltpu.get_barrier_semaphore()
    peers = [(f_z, t), (f_core, t), (at_y(f, 1), t), (at_y(f, -1), t)]
    peers += [(f, tensor_at(dx, 0)) for dx in (1, 2, 3)] + [(f, tensor_at(0, dz)) for dz in (1, 2, 3)]
    for peer in peers:
        pl.semaphore_signal(barrier, inc=1, device_id=peer, device_id_type=MESH)
    pltpu.make_async_copy(x_in, x_own, local_sem.at[0]).start()
    pltpu.make_async_copy(gain1_in, gain1, local_sem.at[1]).start()
    pltpu.make_async_copy(gain2_in, gain2, local_sem.at[2]).start()
    for b, (qkv, up, out, down) in enumerate(((qkv1, up1, out1, down1), (qkv2, up2, out2, down2))):
        for ref, at, width in [(qkv.at[j], 128 * j, 128) for j in range(3)] + [(up, 384, 256), (out, 640, 128), (down, 768, 256)]:
            pltpu.make_async_copy(ref, w.at[b, f, :, pl.ds(at, width)], local_sem.at[3 + b]).start()

    def placed(ref, k):
        pltpu.make_async_copy(ref, ref, local_sem.at[k]).wait()

    placed(x_own, 0)
    placed(w.at[0, f], 3)
    xs[t] = jnp.dot(part_order(0), x_own[...], preferred_element_type=F32).astype(BF)
    pl.semaphore_wait(barrier, len(peers))

    used = [0, 0]

    def piece(b, i, slot):
        rows = 64 // PIECES[b]
        return w.at[b, slot, pl.ds(i * rows, rows), :]

    def w_sem(b, i, kind):
        return w_late.at[i, kind] if b else w_early.at[i, kind]

    def w_push(b, i, slot, target, kind=None):
        used[b] += 1
        send(piece(b, i, slot), piece(b, i, slot), w_send.at[b], w_last.at[b] if kind is None else w_sem(b, i, kind), (target, t))

    def w_first(b, i):
        w_push(b, i, f, f_z, 4)
        w_push(b, i, f, at_y(f, 1), 0)
        w_push(b, i, f, at_y(f, -1), 0)
        w_push(b, i, f, f_core)

    def w_rank(b, i, own, k):
        base = f if own else f_z
        early = b == 1 or i < PIECES[b] // 2
        kind = k - 1 if own else 4 + k
        rows = 64 // PIECES[b]
        both = k in (1, 2, 3)
        arrived(w.at[b, pl.ds(0, 2), pl.ds(0, rows), :] if both else piece(b, i, at_y(base, k)), w_sem(b, i, kind))
        for r in (-k, k) if both else (k,):
            slot = at_y(base, r)
            if own or early:
                if r in (-2, -1, 0):
                    w_push(b, i, slot, at_y(f, 1), kind + 1)
                if r in (0, 1, 2):
                    w_push(b, i, slot, at_y(f, -1), kind + 1)
                if early and r == (-3 if own else 3):
                    w_push(b, i, slot, at_y(f, 1 if own else -1), kind + 1)
            if own and not early:
                if r == 3:
                    w_push(b, i, at_y(f, -3 + 6 * odd), at_y(f, 1 - 2 * odd), kind + 1)
                w_push(b, i, slot, f_z, 4 + k)
            w_push(b, i, slot, f_core)

    def w_core(b):
        arrived(w.at[b, pl.ds(0, 16)], w_last.at[b])

    def gather_push(view, k, dx, dz, to_dx, to_dz):
        slot = view.at[tensor_at(4 - dx, 4 - dz)]
        send(slot, slot, ag_send.at[k], ag_recv.at[k, to_dz], (f, tensor_at(to_dx, to_dz)))

    def gather_own(view, k):
        for dz in (1, 3, 2):
            gather_push(view, k, 0, 0, 0, dz)
        for dx in (2, 1, 3):
            gather_push(view, k, 0, 0, dx, 0)

    def gather_forward(view, k, dz):
        arrived(view.at[tensor_at(0, 4 - dz)], ag_recv.at[k, dz])
        for dx in (2, 1, 3):
            gather_push(view, k, 0, dz, dx, 0)

    def gather_rest(view, k):
        arrived(view.at[pl.ds(0, 12)], ag_recv.at[k, 0])

    def normalize(view, rows, gain):
        total = view[0].astype(F32)
        for i in range(1, 16):
            total += view[i].astype(F32)
        mean = jnp.sum(total, axis=-1, keepdims=True) * (1.0 / 2048)
        square = jnp.zeros((rows, 128), F32)
        for i in range(16):
            centered = view[i].astype(F32) - mean
            square += centered * centered
        scale = lax.rsqrt(jnp.sum(square, axis=-1, keepdims=True) * (1.0 / 2048) + EPS)
        for i in range(16):
            centered = view[i].astype(F32) - mean
            h[0:rows, 128 * i : 128 * (i + 1)] = (centered * scale * gain[i]).astype(BF)

    def inner(b, rows):
        mixed = jnp.dot(h[0:rows, :], w[b, :, :, 0:640].reshape(2048, 640), preferred_element_type=F32)
        query = norm_rows(mixed[:, 0:128]).astype(BF)
        keys = norm_rows(mixed[:, 128:256]).astype(BF)
        scores = lax.dot_general(query, keys, NT, preferred_element_type=F32) * 128**-0.5
        expo = jnp.exp(scores)
        if b == 1:
            row = lax.broadcasted_iota(jnp.int32, (rows, 1), 0)
            col = lax.broadcasted_iota(jnp.int32, (1, rows), 1)
            expo = jnp.where((row & (EACH - 1)) == (col & (EACH - 1)), expo, 0.0)
        weights = (expo * (1.0 / jnp.sum(expo, axis=-1, keepdims=True))).astype(BF)
        attended = jnp.dot(weights, mixed[:, 256:384].astype(BF), preferred_element_type=F32).astype(BF)
        hidden = jax.nn.gelu(mixed[:, 384:640], approximate=True).astype(BF)
        return jnp.concatenate([attended, hidden], axis=1)

    order = (2, 1, 3, 0)

    def project(b, k, dz, both):
        for dx in (2, 1, 3, 0):
            slot = 2 * tensor_at(dx, dz)
            weight = w[b, pl.ds(slot, 2), :, 640:1024].reshape(128, 384)
            terms[b, k, dx, dz] = lax.dot_general(both, weight, NT, preferred_element_type=F32).astype(BF)
            if dx:
                send(terms.at[b, k, dx, dz], from_x.at[b, k, dz, dx - 1], rx_send.at[0], rx_recv.at[b, k, dz], (f, tensor_at(dx, 0)))

    def sum_x(b, k, dz):
        arrived(from_x.at[b, k, dz], rx_recv.at[b, k, dz])
        total = terms[b, k, 0, dz].astype(F32)
        for i in range(3):
            total += from_x[b, k, dz, i].astype(F32)
        if dz:
            to_z[b, k, dz - 1] = total.astype(BF)
            send(to_z.at[b, k, dz - 1], from_z.at[b, k, dz - 1], rz_send.at[0], rz_recv.at[b, k], (f, tensor_at(0, dz)))
        else:
            ready[b, k] = total

    def sum_z(b, k):
        arrived(from_z.at[b, k], rz_recv.at[b, k])
        total = ready[b, k]
        for i in range(3):
            total += from_z[b, k, i].astype(F32)
        return total

    distances = sorted(range(1, 32), key=lambda i: -min(i // 4, 8 - i // 4))

    def turn(k):
        middle = (xs[t, k * ROWS : (k + 1) * ROWS, :].astype(F32) + sum_z(0, k)).astype(BF).astype(F32)
        mid[k] = middle.reshape(32, EACH, 128)
        for i in distances:
            to = (f + i) % 32
            send(mid.at[k, to], turned.at[k, f], turn_send.at[k], turn_recv.at[k], (to, t))
        turned[k, f] = mid[k, f]

    def turn_done(k):
        arrived(turned.at[k, pl.ds(0, 31)], turn_recv.at[k])
        xt[k, t] = turned[k].reshape(ROWS, 128).astype(BF)

    pieces = range(PIECES[0])
    early, late = pieces[: PIECES[0] // 2], pieces[PIECES[0] // 2 :]
    for i in pieces:
        w_first(0, i)
    gather_own(xs, 0)
    for i in pieces:
        w_rank(0, i, True, 1)
    for i in pieces:
        w_rank(0, i, False, 0)
    for i in early:
        w_rank(0, i, True, 2)
    gather_forward(xs, 0, 3 - 2 * lo)
    for i in late:
        w_rank(0, i, True, 2)
    for i in pieces:
        w_rank(0, i, False, 1)
    for i in early:
        w_rank(0, i, True, 3)
    gather_forward(xs, 0, 1 + 2 * lo)
    for i in late:
        w_rank(0, i, True, 3)
    gather_forward(xs, 0, 2)
    for i in (*late, *early):
        w_rank(0, i, False, 2)
    for i in pieces:
        w_rank(0, i, True, 4)
    for i in (*late, *early):
        w_rank(0, i, False, 3)
    for i in late:
        w_rank(0, i, False, 4)
    gather_rest(xs, 0)
    placed(gain1, 1)
    normalize(xs, 256, gain1)
    for i in early:
        w_rank(0, i, False, 4)

    w_core(0)
    branches = {}
    entered = inner(0, 256)
    for k in range(PARTS):
        branches[0, k] = entered[k * ROWS : (k + 1) * ROWS]
    placed(w.at[1, f], 4)
    placed(gain2, 2)

    for step, *at in PLAN:
        if step == "first":
            for i in range(PIECES[1]):
                w_first(1, i)
        elif step == "weight":
            w_rank(1, *at)
        elif step == "project":
            project(*at, branches[at[0], at[1]])
        elif step == "sum":
            sum_x(*at)
        elif step == "turn":
            turn(*at)
        elif step == "turned":
            turn_done(*at)
            gather_own(xt.at[at[0]], at[0] + 1)
        elif step == "forward":
            gather_forward(xt.at[at[0]], at[0] + 1, at[1])
        elif step == "enter":
            k = at[0]
            gather_rest(xt.at[k], k + 1)
            normalize(xt.at[k], ROWS, gain2)
            if k == 0:
                w_core(1)
            branches[1, k] = inner(1, ROWS)
    total = jnp.concatenate([sum_z(1, k) for k in range(PARTS)], axis=0)
    kept = jnp.concatenate([turned[k].reshape(ROWS, 128) for k in range(PARTS)], axis=0)
    y_out[...] = jnp.dot(part_order(1), (kept + total).astype(BF), preferred_element_type=F32).astype(BF)
    for b in range(2):
        left(w.at[b, pl.ds(0, used[b] // PIECES[b])], w_send.at[b])
    left(xs.at[pl.ds(0, 15)], ag_send.at[0])
    for k in range(PARTS):
        left(xt.at[k, pl.ds(0, 15)], ag_send.at[k + 1])
        left(mid.at[k, pl.ds(0, 31)], turn_send.at[k])
    left(from_x, rx_send.at[0])
    left(to_z, rz_send.at[0])


def body(
    frames_in,
    spatial_gain,
    spatial_qkv,
    spatial_out,
    spatial_up,
    spatial_down,
    temporal_gain,
    temporal_qkv,
    temporal_out,
    temporal_up,
    temporal_down,
):
    dma = pltpu.SemaphoreType.DMA
    result = pl.pallas_call(
        kernel,
        out_shape=jax.ShapeDtypeStruct((256, 128), BF),
        in_specs=[pl.BlockSpec(memory_space=pl.ANY)] * 11,
        out_specs=pl.BlockSpec(memory_space=pltpu.VMEM),
        scratch_shapes=[
            pltpu.VMEM((2, 32, 64, 1024), BF),
            pltpu.VMEM((16, 1, 128), F32),
            pltpu.VMEM((16, 1, 128), F32),
            pltpu.VMEM((256, 128), BF),
            pltpu.VMEM((16, 256, 128), BF),
            pltpu.VMEM((PARTS, 16, ROWS, 128), BF),
            pltpu.VMEM((256, 2048), BF),
            pltpu.VMEM((2, PARTS, 4, 4, ROWS, 128), BF),
            pltpu.VMEM((2, PARTS, 4, 3, ROWS, 128), BF),
            pltpu.VMEM((2, PARTS, 3, ROWS, 128), BF),
            pltpu.VMEM((2, PARTS, 3, ROWS, 128), BF),
            pltpu.VMEM((PARTS, 32, EACH, 128), F32),
            pltpu.VMEM((PARTS, 32, EACH, 128), F32),
            pltpu.VMEM((2, PARTS, ROWS, 128), F32),
            dma((5,)),
            dma((2,)),
            dma((PIECES[0], 9)),
            dma((PIECES[1], 9)),
            dma((2,)),
            dma((1 + PARTS,)),
            dma((1 + PARTS, 4)),
            dma((2,)),
            dma((2, PARTS, 4)),
            dma((1,)),
            dma((2, PARTS)),
            dma((PARTS,)),
            dma((PARTS,)),
        ],
        compiler_params=pltpu.CompilerParams(collective_id=0, has_side_effects=True, vmem_limit_bytes=63 << 20),
    )(
        frames_in.reshape(256, 128),
        spatial_gain.reshape(16, 1, 128),
        temporal_gain.reshape(16, 1, 128),
        jnp.transpose(spatial_qkv, (1, 0, 2)),
        spatial_out,
        spatial_up,
        spatial_down,
        jnp.transpose(temporal_qkv, (1, 0, 2)),
        temporal_out,
        temporal_up,
        temporal_down,
    )
    return result.reshape(32, 8, 128)


def solution(mesh):
    in_specs = (
        P("frame", None, "tensor"),
        P(),
        P("frame", None, "tensor"),
        P("frame", "tensor"),
        P("frame", "tensor"),
        P("frame", "tensor"),
        P(),
        P("frame", None, "tensor"),
        P("frame", "tensor"),
        P("frame", "tensor"),
        P("frame", "tensor"),
    )
    out_specs = P(None, "frame", "tensor")
    return jax.shard_map(body, mesh=mesh, in_specs=in_specs, out_specs=out_specs, check_vma=False)
```
